128 devices in a mesh: row: 16 (over y, x), col: 8 (over z, core).
Axes of the slice: x: 4, y: 4, z: 4, core: 2. Of those that a mesh axis runs over, the one named last changes fastest.
Arguments:
- tokens: bfloat16 [8192, 3072], P('row', 'col'), may hold values from -6 to 6
- weight: bfloat16 [3072, 12288], P('row', 'col'), may hold values from -0.109375 to 0.109375
- cotangent: bfloat16 [8192, 12288], P('row', 'col'), may hold values from -6 to 6
Outputs:
- activated: bfloat16 [8192, 12288], P('row', 'col')
- input_grad: bfloat16 [8192, 3072], P('row', 'col')
- weight_grad: float32 [3072, 12288], P('row', 'col')
The draws below stay inside these ranges and needn't reach their ends.
All inputs are finite; a program needn't handle non-finite values.
Results may differ from the reference program's by a relative error of at most 0.0049.
Values may be sent and summed in bfloat16 or wider, within the bound.
No kernel may reach another device: no remote copies, remote signals or barrier semaphores. Data moves between devices by JAX's collectives and lax.ppermute only.
A program may use at most 128 MiB of HBM per device.

```python
import jax
import jax.numpy as jnp
from jax import lax

D = 3072
FF = 12288
TOKENS = 8192


def raised(entries, stream_key, source, target, parts, factor):
    owner, partner = [(jnp.arange(entries.shape[dim]) // (entries.shape[dim] // parts)).reshape([-1 if axis == dim else 1 for axis in range(entries.ndim)]) for dim in (source, target)]
    chosen = jax.random.permutation(stream_key, parts)[partner]
    strong = (owner == chosen) | (owner == (partner + parts // 2) % parts)
    return jnp.where(strong, factor * entries, entries)


def levels(rng, extent, split, smallest, high):
    def one(axis_at, blocks):
        steps = jax.random.uniform(jax.random.fold_in(jax.random.fold_in(rng, 6), axis_at), (blocks,), jnp.float32, smallest / len(split), high / len(split))
        return jnp.repeat(jnp.exp(steps), extent[axis_at] // blocks).reshape((-1,) + (1,) * (len(extent) - axis_at - 1))

    loudness = one(*split[0])
    for cut in split[1:]:
        loudness = loudness * one(*cut)
    return loudness


def centred(stream_key, dims, width, bound, cuts=(), dtype=jnp.bfloat16):
    level = levels(stream_key, dims, cuts, -0.22, 0.18) if cuts else 1.0
    entries = jax.random.normal(stream_key, dims, jnp.float32) * width * level
    return jnp.minimum(jnp.maximum(entries, -bound), bound).astype(dtype)


def bell_draw_with(rng, shape, deviation, limit, split, heavy, held_as=jnp.bfloat16):
    result = deviation * jax.random.normal(rng, shape, jnp.float32)
    if split:
        result = result * levels(rng, shape, split, -0.22, 0.18)
    return jnp.clip(raised(result, jax.random.fold_in(rng, 3), *heavy), -limit, limit).astype(held_as)


def setup_inputs(seed: int = 0) -> dict:
    seeds = jax.random.split(jax.random.key(seed), 4)
    return {
        "tokens": bell_draw_with(seeds[0], (TOKENS, D), 1.0, 6.0, ((0, 16), (1, 8)), (0, 1, 16, 2.0)),
        "weight": centred(seeds[1], (D, FF), D ** -0.5, 0.109375, ((0, 16), (1, 8))),
        "cotangent": centred(seeds[2], (TOKENS, FF), 1.0, 6.0, ((0, 16), (1, 8))),
    }


def gelu_tanh(value):
    return jax.nn.gelu(value, approximate=True)

def reference(tokens, weight, cotangent):
    pre = jnp.dot(tokens, weight, preferred_element_type=jnp.float32)
    outputs, pullback = jax.vjp(gelu_tanh, pre)
    activated = outputs.astype(jnp.bfloat16)
    grad_pre = pullback(cotangent.astype(jnp.float32))[0].astype(jnp.bfloat16)
    input_grad = lax.dot_general(grad_pre, weight, (((1,), (1,)), ((), ())), preferred_element_type=jnp.float32).astype(jnp.bfloat16)
    weight_grad = lax.dot_general(tokens, grad_pre, (((0,), (0,)), ((), ())), preferred_element_type=jnp.float32)
    return (activated, input_grad, weight_grad)
```

```python
import jax
import jax.numpy as jnp
from jax import lax
from jax.sharding import PartitionSpec as P

N = 4
BF = jnp.bfloat16


def gelu_tanh(value):
    return jax.nn.gelu(value, approximate=True)


def shift_x(block, step):
    pairs = [(y * N + x, y * N + (x + step) % N) for y in range(N) for x in range(N)]
    return lax.ppermute(block, "row", pairs)


def shift_y(block, step):
    pairs = [(y * N + x, (y + step) % N * N + x) for y in range(N) for x in range(N)]
    return lax.ppermute(block, "row", pairs)


def gather(block, small, big):
    halves = (
        jnp.stack([block, small(block, -1)]),
        jnp.stack([small(block, 2), small(block, 1)]),
    )
    up_low = big(halves[0], -1)
    down_high = big(halves[1], 1)
    up_high = big(halves[1], -1)
    down_low = big(halves[0], 1)
    far_low = big(up_low, -1)
    far_high = big(down_high, 1)
    return [halves, (up_low, up_high), (far_low, far_high), (down_low, down_high)]


def scatter(part, small, big):
    far_low = part(2, 0).astype(BF)
    far_high = part(2, 1).astype(BF)
    to_up = big(far_low, 1)
    to_down = big(far_high, -1)
    up_high = big(part(1, 1).astype(BF), 1)
    down_low = big(part(3, 0).astype(BF), -1)
    up_low = big((part(1, 0) + to_up.astype(jnp.float32)).astype(BF), 1)
    down_high = big((part(3, 1) + to_down.astype(jnp.float32)).astype(BF), -1)
    low = part(0, 0) + up_low.astype(jnp.float32) + down_low.astype(jnp.float32)
    high = part(0, 1) + up_high.astype(jnp.float32) + down_high.astype(jnp.float32)
    out = low[0]
    out = out + small(low[1].astype(BF), 1).astype(jnp.float32)
    out = out + small(high[0].astype(BF), 2).astype(jnp.float32)
    out = out + small(high[1].astype(BF), -1).astype(jnp.float32)
    return out


def dot(a, b, ca, cb):
    return lax.dot_general(a, b, (((ca,), (cb,)), ((), ())), preferred_element_type=jnp.float32)


def shards(tokens, weight, cotangent):
    place = lax.axis_index("row")
    y, x = place // N, place % N
    features = lax.all_gather(tokens.T, "col", axis=0, tiled=True)
    depth, count = weight.shape[0], tokens.shape[0]
    half = weight.shape[1] // 2
    blocks = features.reshape(N, N, depth, count)
    doubled = jnp.concatenate([blocks, blocks], axis=0)
    blocks = lax.dynamic_slice_in_dim(doubled, y, N, axis=0)
    doubled = jnp.concatenate([blocks, blocks], axis=1)
    rel = lax.dynamic_slice_in_dim(doubled, x, N, axis=1)

    wide = lambda i, h: rel[i, 2 * h : 2 * h + 2].reshape(2 * depth, count)
    tall = lambda i, h: rel[2 * h : 2 * h + 2, i].reshape(2 * depth, count)

    w_a = gather(weight[:, :half], shift_x, shift_y)
    w_b = gather(weight[:, half:], shift_y, shift_x)

    def forward(panel, pick, cot):
        pre = 0.0
        for i in (0, 1, 3, 2):
            for h in (0, 1):
                pre = pre + dot(pick(i, h), panel[i][h].reshape(2 * depth, half), 0, 0)
        outputs, pullback = jax.vjp(gelu_tanh, pre)
        return outputs.astype(BF), pullback(cot.astype(jnp.float32))[0].astype(BF)

    act_a, g_a = forward(w_a, wide, cotangent[:, :half])
    act_b, g_b = forward(w_b, tall, cotangent[:, half:])

    grad_a = scatter(lambda i, h: dot(wide(i, h), g_a, 1, 0).reshape(2, depth, half), shift_x, shift_y)
    grad_b = scatter(lambda i, h: dot(tall(i, h), g_b, 1, 0).reshape(2, depth, half), shift_y, shift_x)

    panel_a = jnp.stack([jnp.concatenate(pair, axis=0) for pair in w_a], axis=0)
    panel_b = jnp.stack([jnp.concatenate(pair, axis=0) for pair in w_b], axis=1)
    panel = jnp.concatenate([panel_a, panel_b], axis=-1)
    g = jnp.concatenate([g_a, g_b], axis=-1)
    partial = dot(panel.reshape(N * N * depth, 2 * half), g, 1, 1).reshape(N, N, depth, count)
    doubled = jnp.concatenate([partial, partial], axis=0)
    partial = lax.dynamic_slice_in_dim(doubled, (N - y) % N, N, axis=0)
    doubled = jnp.concatenate([partial, partial], axis=1)
    partial = lax.dynamic_slice_in_dim(doubled, (N - x) % N, N, axis=1).reshape(N * N * depth, count)
    input_grad = lax.psum_scatter(partial, "col", scatter_dimension=0, tiled=True).T.astype(BF)

    return (
        jnp.concatenate([act_a, act_b], axis=1),
        input_grad,
        jnp.concatenate([grad_a, grad_b], axis=1),
    )


def solution(mesh):
    specs = (P("row", "col"), P("row", "col"), P("row", "col"))
    return jax.shard_map(shards, mesh=mesh, in_specs=specs, out_specs=specs, check_vma=False)
```

```python
import jax
import jax.numpy as jnp
from jax import lax
from jax.experimental import pallas as pl
from jax.experimental.pallas import tpu as pltpu
from jax.sharding import PartitionSpec as P

N = 4
BF = jnp.bfloat16
F32 = jnp.float32


def gelu_tanh(value):
    return jax.nn.gelu(value, approximate=True)


def shift_x(block, step):
    pairs = [(y * N + x, y * N + (x + step) % N) for y in range(N) for x in range(N)]
    return lax.ppermute(block, "row", pairs)


def shift_y(block, step):
    pairs = [(y * N + x, (y + step) % N * N + x) for y in range(N) for x in range(N)]
    return lax.ppermute(block, "row", pairs)


def swap_core(block):
    pairs = [(col, col ^ 1) for col in range(2 * N)]
    return lax.ppermute(block, "col", pairs)


def tied(*values):
    return lax.optimization_barrier(values)


def dot(a, b, ca, cb):
    return lax.dot_general(a, b, (((ca,), (cb,)), ((), ())), preferred_element_type=F32)


def input_kernel(place, _, g_a, g_b, *refs):
    pieces_a, pieces_b, out = refs[:8], refs[8:16], refs[16]
    turned_a, turned_b, held, sems = refs[17:]
    depth = held.shape[1]
    turned_a[...] = g_a[...].T
    turned_b[...] = g_b[...].T
    slots = held.shape[0]
    copies = []
    for k in range(N * N):
        i, j = divmod(k, N)
        if k >= slots:
            copies[k - slots].wait()
        total = jnp.dot(pieces_a[2 * i + j // 2][j % 2], turned_a[...], preferred_element_type=F32)
        total += jnp.dot(pieces_b[2 * j + i // 2][i % 2], turned_b[...], preferred_element_type=F32)
        held[k % slots] = total
        row = lax.rem(place[0] + i, N) * N + lax.rem(place[1] + j, N)
        copies.append(
            pltpu.make_async_copy(
                held.at[k % slots],
                out.at[pl.ds(pl.multiple_of(row * depth, depth), depth)],
                sems.at[k % slots],
            )
        )
        copies[k].start()
    for k in range(N * N - slots, N * N):
        copies[k].wait()


def input_partial(place, first, g_a, g_b, pieces_a, pieces_b):
    count, half = g_a.shape
    depth = pieces_a[0].shape[1]
    vmem = pl.BlockSpec(memory_space=pltpu.VMEM)
    return pl.pallas_call(
        input_kernel,
        out_shape=jax.ShapeDtypeStruct((N * N * depth, count), F32),
        in_specs=[pl.BlockSpec(memory_space=pltpu.SMEM)] + [vmem] * 19,
        out_specs=pl.BlockSpec(memory_space=pl.ANY),
        scratch_shapes=[
            pltpu.VMEM((half, count), BF),
            pltpu.VMEM((half, count), BF),
            pltpu.VMEM((4, depth, count), F32),
            pltpu.SemaphoreType.DMA((4,)),
        ],
        compiler_params=pltpu.CompilerParams(vmem_limit_bytes=40 * 2**20),
        cost_estimate=pl.CostEstimate(
            flops=4 * N * N * depth * half * count, bytes_accessed=8 * 2**20, transcendentals=0
        ),
    )(place, first, g_a, g_b, *pieces_a, *pieces_b)


def shards(tokens, weight, cotangent):
    place = lax.axis_index("row")
    y, x = place // N, place % N
    features = lax.all_gather(tokens.T, "col", axis=0, tiled=True)
    depth, count = weight.shape[0], tokens.shape[0]
    half = weight.shape[1] // 2
    blocks = features.reshape(N, N, depth, count)
    doubled = jnp.concatenate([blocks, blocks], axis=0)
    blocks = lax.dynamic_slice_in_dim(doubled, y, N, axis=0)
    doubled = jnp.concatenate([blocks, blocks], axis=1)
    rel = lax.dynamic_slice_in_dim(doubled, x, N, axis=1)

    def wide(i, h):
        return rel[i, 2 * h : 2 * h + 2].reshape(2 * depth, count)

    def tall(i, h):
        return rel[2 * h : 2 * h + 2, i].reshape(2 * depth, count)

    a0, b0 = weight[:, :half], weight[:, half:]
    a1, b1 = shift_x(a0, -1), shift_y(b0, -1)
    a3, b3 = shift_x(a0, 1), shift_y(b0, 1)
    a2, b2 = shift_x(a0, 2), shift_y(b0, 2)
    low_a, low_b = jnp.stack([a0, a1]), jnp.stack([b0, b1])
    high_a, high_b = jnp.stack([a2, a3]), jnp.stack([b2, b3])
    up_low_a = shift_y(low_a, -1)
    down_low_a = shift_y(low_a, 1)
    up_low_b = shift_x(low_b, -1)
    down_low_b = shift_x(low_b, 1)
    up_high_a = shift_y(high_a, -1)
    late_high_a, up_low_a = tied(high_a, up_low_a)
    down_high_a = shift_y(late_high_a, 1)
    late_high_b, down_low_a = tied(high_b, down_low_a)
    up_high_b = shift_x(late_high_b, -1)
    late_high_b, up_low_b = tied(high_b, up_low_b)
    down_high_b = shift_x(late_high_b, 1)
    late, down_low_b = tied(up_low_a, down_low_b)
    far_low_a = shift_y(late, -1)
    late, up_high_a, rel = tied(up_low_b, up_high_a, rel)
    far_low_b = shift_x(late, -1)
    far_high_a = shift_y(down_high_a, 1)
    far_high_b = shift_x(down_high_b, 1)
    w_a = [low_a, high_a, up_low_a, up_high_a, far_low_a, far_high_a, down_low_a, down_high_a]
    w_b = [low_b, high_b, up_low_b, up_high_b, far_low_b, far_high_b, down_low_b, down_high_b]

    def forward(panel, pick, cot):
        pre = 0.0
        for k in (0, 1, 2, 6, 3, 7):
            pre = pre + dot(pick(k // 2, k % 2), panel[k].reshape(2 * depth, half), 0, 0)
        for k in (4, 5):
            pre = pre + dot(pick(k // 2, k % 2), panel[k].reshape(2 * depth, half), 0, 0)
        outputs, pullback = jax.vjp(gelu_tanh, pre)
        return outputs.astype(BF), pullback(cot.astype(F32))[0].astype(BF)

    act_a, g_a = forward(w_a, wide, cotangent[:, :half])
    act_b, g_b = forward(w_b, tall, cotangent[:, half:])

    def part_a(i, h):
        return dot(wide(i, h), g_a, 1, 0).reshape(2, depth, half)

    def part_b(i, h):
        return dot(tall(i, h), g_b, 1, 0).reshape(2, depth, half)

    to_up_a = shift_y(part_a(2, 0).astype(BF), 1)
    to_down_a = shift_y(part_a(2, 1).astype(BF), -1)
    to_up_b = shift_x(part_b(2, 0).astype(BF), 1)
    last_b = part_b(2, 1).astype(BF)
    to_down_b = shift_x(last_b, -1)
    small = swap_core(last_b[0, :16, :128])
    up_high_a = shift_y(part_a(1, 1).astype(BF), 1)
    late, to_up_a = tied(part_a(3, 0).astype(BF), to_up_a)
    down_low_a = shift_y(late, -1)
    late, to_down_a = tied(part_b(1, 1).astype(BF), to_down_a)
    up_high_b = shift_x(late, 1)
    late, to_up_b = tied(part_b(3, 0).astype(BF), to_up_b)
    down_low_b = shift_x(late, -1)
    late, to_down_b = tied((part_a(1, 0) + to_up_a.astype(F32)).astype(BF), to_down_b)
    up_low_a = shift_y(late, 1)
    late, up_high_a = tied((part_a(3, 1) + to_down_a.astype(F32)).astype(BF), up_high_a)
    down_high_a = shift_y(late, -1)
    late, down_low_a = tied((part_b(1, 0) + to_up_b.astype(F32)).astype(BF), down_low_a)
    up_low_b = shift_x(late, 1)
    late, up_high_b = tied((part_b(3, 1) + to_down_b.astype(F32)).astype(BF), up_high_b)
    down_high_b = shift_x(late, -1)

    partial = input_partial(jnp.stack([y, x]), small, g_a, g_b, w_a, w_b)
    input_grad = lax.psum_scatter(partial, "col", scatter_dimension=0, tiled=True).T.astype(BF)

    high_a = part_a(0, 1) + up_high_a.astype(F32) + down_high_a.astype(F32)
    a3 = shift_x(high_a[1].astype(BF), -1)
    a2 = shift_x(high_a[0].astype(BF), 2)
    low_a = part_a(0, 0) + up_low_a.astype(F32) + down_low_a.astype(F32)
    a1 = shift_x(low_a[1].astype(BF), 1)
    high_b = part_b(0, 1) + up_high_b.astype(F32) + down_high_b.astype(F32)
    b3 = shift_y(high_b[1].astype(BF), -1)
    b2 = shift_y(high_b[0].astype(BF), 2)
    low_b = part_b(0, 0) + up_low_b.astype(F32) + down_low_b.astype(F32)
    b1 = shift_y(low_b[1].astype(BF), 1)
    grad_a = low_a[0] + a1.astype(F32) + a2.astype(F32) + a3.astype(F32)
    grad_b = low_b[0] + b1.astype(F32) + b2.astype(F32) + b3.astype(F32)

    return (
        jnp.concatenate([act_a, act_b], axis=1),
        input_grad,
        jnp.concatenate([grad_a, grad_b], axis=1),
    )


def solution(mesh):
    specs = (P("row", "col"), P("row", "col"), P("row", "col"))
    return jax.shard_map(shards, mesh=mesh, in_specs=specs, out_specs=specs, check_vma=False)
```

```python
import functools

import jax
import jax.numpy as jnp
from jax import lax
from jax.experimental import pallas as pl
from jax.experimental.pallas import tpu as pltpu
from jax.sharding import PartitionSpec as P

N = 4
BF = jnp.bfloat16
F32 = jnp.float32


def shift(block, step, first):
    pairs = []
    for y in range(N):
        for x in range(N):
            for col in range(2 * N):
                if first == (col % 2 == 0):
                    to = y * N + (x + step) % N
                else:
                    to = (y + step) % N * N + x
                pairs.append(((y * N + x) * 2 * N + col, to * 2 * N + col))
    return lax.ppermute(block, ("row", "col"), pairs)


def small(block, step):
    return shift(block, step, True)


def big(block, step):
    return shift(block, step, False)


def shift_z(block, step):
    pairs = [(2 * z + core, 2 * ((z + step) % N) + core) for z in range(N) for core in range(2)]
    return lax.ppermute(block, "col", pairs)


def swap_core(block):
    pairs = [(col, col ^ 1) for col in range(2 * N)]
    return lax.ppermute(block, "col", pairs)


def tied(*values):
    return lax.optimization_barrier(values)


def dot(a, b, ca, cb):
    return lax.dot_general(a, b, (((ca,), (cb,)), ((), ())), preferred_element_type=F32)


def whole(count):
    return [pl.BlockSpec(memory_space=pltpu.VMEM)] * count


def limits(flops, moved, transcendentals=0):
    return dict(
        compiler_params=pltpu.CompilerParams(vmem_limit_bytes=48 * 2**20),
        cost_estimate=pl.CostEstimate(
            flops=flops, bytes_accessed=moved, transcendentals=transcendentals
        ),
    )


def turn_kernel(source, out):
    out[...] = source[...].T


def turn(block):
    return pl.pallas_call(
        turn_kernel,
        out_shape=jax.ShapeDtypeStruct(block.shape[::-1], block.dtype),
        in_specs=whole(1),
        out_specs=whole(1)[0],
        **limits(0, 4 * block.size),
    )(block)


def chip(place, i, j):
    turned = place[3] == 1
    y = lax.rem(place[0] + jnp.where(turned, j, i), N)
    x = lax.rem(place[1] + jnp.where(turned, i, j), N)
    return y * N + x, y, x


def order_kernel(place, source, out, sem):
    depth = out.shape[2]
    copies = []
    for i in range(N):
        for j in range(N):
            row, _, _ = chip(place, i, j)
            copies.append(
                pltpu.make_async_copy(
                    source.at[pl.ds(pl.multiple_of(row * depth, depth), depth)], out.at[i, j], sem.at[i, j]
                )
            )
            copies[-1].start()
    for copy in copies:
        copy.wait()


def ordered(place, features):
    rows, count = features.shape
    return pl.pallas_call(
        order_kernel,
        out_shape=jax.ShapeDtypeStruct((N, N, rows // (N * N), count), features.dtype),
        in_specs=[pl.BlockSpec(memory_space=pltpu.SMEM), pl.BlockSpec(memory_space=pl.ANY)],
        out_specs=whole(1)[0],
        scratch_shapes=[pltpu.SemaphoreType.DMA((N, N))],
        **limits(0, 4 * features.size),
    )(place, features)


def add_pieces(total, rel, pieces, tokens):
    for (i, h), piece in pieces.items():
        left = rel[i, 2 * h : 2 * h + 2, :, tokens]
        term = dot(left.reshape(-1, left.shape[-1]), piece[...].reshape(-1, piece.shape[-1]), 0, 0)
        total = term if total is None else total + term
    return total


STEP = 128


def sum_kernel(keys, has_first, rel, *refs):
    first = refs[0] if has_first else None
    pieces = dict(zip(keys, refs[has_first : has_first + len(keys)]))
    out = refs[-1]
    for at in range(0, out.shape[0], STEP):
        tokens = slice(at, at + STEP)
        out[tokens] = add_pieces(first[tokens] if has_first else None, rel, pieces, tokens)


def add_sums(rel, first, pieces):
    shape = (rel.shape[-1], next(iter(pieces.values())).shape[-1])
    firsts = () if first is None else (first,)
    return pl.pallas_call(
        functools.partial(sum_kernel, tuple(pieces), len(firsts)),
        out_shape=jax.ShapeDtypeStruct(shape, F32),
        in_specs=whole(1 + len(firsts) + len(pieces)),
        out_specs=whole(1)[0],
        **limits(4 * shape[0] * rel.shape[2] * shape[1] * len(pieces), 12 * 2**20),
    )(rel, *firsts, *pieces.values())


def late_kernel(keys, rel, sums, cot, *refs):
    pieces = dict(zip(keys, refs))
    activated, grad = refs[len(keys) :]
    for at in range(0, sums.shape[0], STEP):
        tokens = slice(at, at + STEP)
        pre = add_pieces(sums[tokens], rel, pieces, tokens)
        square = pre * pre
        bend = jnp.tanh(0.7978845608028654 * (pre + 0.044715 * (square * pre)))
        rise = 0.5 + 0.5 * bend
        activated[tokens] = (pre * rise).astype(BF)
        slope = rise + 0.5 * pre * (1.0 - bend * bend) * (
            0.7978845608028654 * (1.0 + 3 * 0.044715 * square)
        )
        grad[tokens] = (cot[tokens].astype(F32) * slope).astype(BF)


def finish(rel, sums, cot, pieces):
    out = jax.ShapeDtypeStruct(sums.shape, BF)
    return pl.pallas_call(
        functools.partial(late_kernel, tuple(pieces)),
        out_shape=(out, out),
        in_specs=whole(3 + len(pieces)),
        out_specs=whole(2),
        **limits(4 * sums.size * rel.shape[2] * len(pieces), 10 * 2**20, sums.size),
    )(rel, sums, cot, *pieces.values())


def input_kernel(keys, place, g, *refs):
    pieces = dict(zip(keys, refs))
    kept, given, turned = refs[len(keys) :]
    turned[...] = g[...].T
    z, core = place[2], place[3]
    for (i, h), piece in pieces.items():
        depth = piece.shape[1]
        for j in (2 * h, 2 * h + 1):
            total = dot(piece[j % 2], turned[...], 1, 0)
            _, ahead, other = chip(place, i, j)
            to = lax.rem(ahead + N - z, N) * 2 + lax.rem(other, 2)
            rows = pl.ds(pl.multiple_of(to * depth, depth), depth)
            mine = other // 2 == core

            @pl.when(mine)
            def _():
                kept[rows] = total

            @pl.when(jnp.logical_not(mine))
            def _():
                given[rows] = total.astype(given.dtype)


def input_partial(place, g, pieces):
    count, width = g.shape
    rows = N * N * pieces[0, 0].shape[1] // 2
    return pl.pallas_call(
        functools.partial(input_kernel, tuple(pieces)),
        out_shape=(jax.ShapeDtypeStruct((rows, count), F32), jax.ShapeDtypeStruct((rows, count), BF)),
        in_specs=[pl.BlockSpec(memory_space=pltpu.SMEM)] + whole(1 + len(pieces)),
        out_specs=tuple(whole(2)),
        scratch_shapes=[pltpu.VMEM((width, count), BF)],
        **limits(4 * rows * width * count, 8 * 2**20),
    )(place, g, *pieces.values())


def shards(tokens, weight, cotangent):
    row, col = lax.axis_index("row"), lax.axis_index("col")
    place = jnp.stack([row // N, row % N, col // 2, col % 2])
    depth, count = weight.shape[0], tokens.shape[0]
    features = lax.all_gather(turn(tokens), "col", axis=0, tiled=True)

    up, down, across = small(weight, -1), small(weight, 1), small(weight, 2)
    w = {(0, 0): jnp.stack([weight, up]), (0, 1): jnp.stack([across, down])}
    w[1, 0] = big(w[0, 0], -1)
    w[3, 1] = big(w[0, 1], 1)
    w[1, 1] = big(w[0, 1], -1)
    w[3, 0] = big(w[0, 0], 1)
    w[1, 0], w[3, 0], features = tied(w[1, 0], w[3, 0], features)
    rel = ordered(place, features)
    sums = add_sums(rel, None, {k: w[k] for k in ((0, 0), (0, 1), (1, 0), (3, 0))})
    w[2, 0] = big(w[1, 0], -1)
    w[2, 1] = big(w[3, 1], 1)
    sums = add_sums(rel, sums, {k: w[k] for k in ((1, 1), (3, 1))})
    activated, g = finish(rel, sums, cotangent, {k: w[k] for k in ((2, 0), (2, 1))})

    def part(i, h):
        block = rel[i, 2 * h : 2 * h + 2].reshape(2 * depth, count)
        return dot(block, g, 1, 0).reshape(2, depth, -1)

    to_up = big(part(2, 0).astype(BF), 1)
    to_down = big(part(2, 1).astype(BF), -1)
    up_high = big(part(1, 1).astype(BF), 1)
    down_low = big(part(3, 0).astype(BF), -1)
    to_up, to_down, later = tied(to_up, to_down, g)
    up_low = big((part(1, 0) + to_up.astype(F32)).astype(BF), 1)
    down_high = big((part(3, 1) + to_down.astype(F32)).astype(BF), -1)
    kept, given = input_partial(place, later, w)
    high = part(0, 1) + up_high.astype(F32) + down_high.astype(F32)
    low = part(0, 0) + up_low.astype(F32) + down_low.astype(F32)
    across = small(high[0].astype(BF), 2)
    up = small(low[1].astype(BF), 1)
    down = small(high[1].astype(BF), -1)
    weight_grad = low[0] + up.astype(F32) + down.astype(F32) + across.astype(F32)

    sums = (kept + swap_core(given).astype(F32)).reshape(N, -1, count)
    sent = sums.astype(BF)
    z1, z3, z2 = shift_z(sent[1], 1), shift_z(sent[3], -1), shift_z(sent[2], 2)
    input_grad = (sums[0] + z1.astype(F32) + z2.astype(F32) + z3.astype(F32)).T.astype(BF)
    return (activated, input_grad, weight_grad)


def solution(mesh):
    specs = (P("row", "col"), P("row", "col"), P("row", "col"))
    return jax.shard_map(shards, mesh=mesh, in_specs=specs, out_specs=specs, check_vma=False)
```

```python
import functools

import jax
import jax.numpy as jnp
from jax import lax
from jax.experimental import pallas as pl
from jax.experimental.pallas import tpu as pltpu
from jax.sharding import PartitionSpec as P

N = 4
BF = jnp.bfloat16
F32 = jnp.float32


def shift(block, step, first):
    pairs = []
    for y in range(N):
        for x in range(N):
            for col in range(2 * N):
                if first == (col % 2 == 0):
                    to = y * N + (x + step) % N
                else:
                    to = (y + step) % N * N + x
                pairs.append(((y * N + x) * 2 * N + col, to * 2 * N + col))
    return lax.ppermute(block, ("row", "col"), pairs)


def small(block, step):
    return shift(block, step, True)


def big(block, step):
    return shift(block, step, False)


def shift_z(block, step):
    pairs = [(2 * z + core, 2 * ((z + step) % N) + core) for z in range(N) for core in range(2)]
    return lax.ppermute(block, "col", pairs)


def spread_z(block):
    pairs = [(2 * z + core, 2 * ((z + 1 - 2 * core) % N) + core) for z in range(N) for core in range(2)]
    return lax.ppermute(block, "col", pairs)


def swap_core(block):
    pairs = [(col, col ^ 1) for col in range(2 * N)]
    return lax.ppermute(block, "col", pairs)


def tied(*values):
    return lax.optimization_barrier(values)


def dot(a, b, ca, cb):
    return lax.dot_general(a, b, (((ca,), (cb,)), ((), ())), preferred_element_type=F32)


def whole(count):
    return [pl.BlockSpec(memory_space=pltpu.VMEM)] * count


def limits(flops):
    return dict(
        compiler_params=pltpu.CompilerParams(vmem_limit_bytes=24 * 2**20),
        cost_estimate=pl.CostEstimate(flops=flops, bytes_accessed=0, transcendentals=0),
    )


def turn_kernel(source, out):
    out[...] = source[...].T


def turn(block):
    return pl.pallas_call(
        turn_kernel,
        out_shape=jax.ShapeDtypeStruct(block.shape[::-1], block.dtype),
        in_specs=whole(1),
        out_specs=whole(1)[0],
        **limits(0),
    )(block)


def chip(place, i, j):
    turned = place[3] == 1
    y = lax.rem(place[0] + jnp.where(turned, j, i), N)
    x = lax.rem(place[1] + jnp.where(turned, i, j), N)
    return y * N + x, y, x


def arrange_kernel(place, here, got, other, out, sems):
    z, core = place[2], place[3]
    depth = out.shape[2]
    copies = []
    for i in range(N):
        for j in range(N):
            _, y, x = chip(place, i, j)
            ahead = lax.rem(y + N - z, N)
            rows = pl.ds(pl.multiple_of(lax.rem(x, 2) * depth, depth), depth)
            swapped = jnp.where(x // 2 == core, 0, 1)
            near = ahead == jnp.where(core == 0, 3, 1)
            two = ahead == 2
            choices = (
                (here, ahead == 0, swapped),
                (got, jnp.logical_or(near, jnp.logical_and(two, swapped == 0)), jnp.where(two, 2, swapped)),
                (
                    other,
                    jnp.logical_or(
                        ahead == jnp.where(core == 0, 1, 3), jnp.logical_and(two, swapped == 1)
                    ),
                    jnp.where(two, 2, 1 - swapped),
                ),
            )
            for source, chosen, at in choices:
                copy = pltpu.make_async_copy(source.at[at, rows], out.at[i, j], sems.at[i, j])
                pl.when(chosen)(copy.start)
            copies.append(pltpu.make_async_copy(here.at[0, rows], out.at[i, j], sems.at[i, j]))
    for copy in copies:
        copy.wait()


def arrange(place, here, got, other):
    _, rows, count = here.shape
    anywhere = pl.BlockSpec(memory_space=pl.ANY)
    return pl.pallas_call(
        arrange_kernel,
        out_shape=jax.ShapeDtypeStruct((N, N, rows // 2, count), BF),
        in_specs=[pl.BlockSpec(memory_space=pltpu.SMEM), anywhere, anywhere, anywhere],
        out_specs=whole(1)[0],
        scratch_shapes=[pltpu.SemaphoreType.DMA((N, N))],
        **limits(0),
    )(place, here, got, other)


def add_pieces(total, rel, pieces, tokens, columns):
    for (i, h), piece in pieces.items():
        left = rel[i, 2 * h : 2 * h + 2, :, tokens]
        right = piece[:, :, columns]
        term = dot(left.reshape(-1, left.shape[-1]), right.reshape(-1, right.shape[-1]), 0, 0)
        total = term if total is None else total + term
    return total


STEP, WIDE = 128, 768


def sum_kernel(keys, has_first, rel, *refs):
    first = refs[0] if has_first else None
    pieces = dict(zip(keys, refs[has_first : has_first + len(keys)]))
    out = refs[-1]
    for at in range(0, out.shape[0], STEP):
        for left in range(0, out.shape[1], WIDE):
            tokens, columns = slice(at, at + STEP), slice(left, left + WIDE)
            before = first[tokens, columns] if has_first else None
            out[tokens, columns] = add_pieces(before, rel, pieces, tokens, columns)


def add_sums(rel, first, pieces):
    shape = (rel.shape[-1], next(iter(pieces.values())).shape[-1])
    firsts = () if first is None else (first,)
    return pl.pallas_call(
        functools.partial(sum_kernel, tuple(pieces), len(firsts)),
        out_shape=jax.ShapeDtypeStruct(shape, F32),
        in_specs=whole(1 + len(firsts) + len(pieces)),
        out_specs=whole(1)[0],
        **limits(0),
    )(rel, *firsts, *pieces.values())


SCALE = 0.7978845608028654


def late_kernel(keys, rel, sums, cot, *refs):
    pieces = dict(zip(keys, refs))
    activated, grad = refs[len(keys) :]
    for at in range(0, sums.shape[0], STEP):
        for left in range(0, sums.shape[1], WIDE):
            tokens, columns = slice(at, at + STEP), slice(left, left + WIDE)
            pre = add_pieces(sums[tokens, columns], rel, pieces, tokens, columns)
            square = pre * pre
            rise = 0.5 + 0.5 * jnp.tanh(pre * (SCALE + (SCALE * 0.044715) * square))
            activated[tokens, columns] = (pre * rise).astype(BF)
            bend = pre * (2 * SCALE + (6 * SCALE * 0.044715) * square)
            slope = rise + rise * ((1.0 - rise) * bend)
            grad[tokens, columns] = (cot[tokens, columns].astype(F32) * slope).astype(BF)


def finish(rel, sums, cot, pieces):
    out = jax.ShapeDtypeStruct(sums.shape, BF)
    return pl.pallas_call(
        functools.partial(late_kernel, tuple(pieces)),
        out_shape=(out, out),
        in_specs=whole(3 + len(pieces)),
        out_specs=whole(2),
        **limits(0),
    )(rel, sums, cot, *pieces.values())


def near_kernel(i, h, rel, g, got, out):
    for j in range(N):
        total = dot(rel[i, j], g[...], 1, 0)
        if j // 2 == h:
            total += got[j % 2].astype(F32)
        out[j] = total.astype(BF)


def near(i, h, rel, g, got):
    depth, width = rel.shape[2], g.shape[1]
    return pl.pallas_call(
        functools.partial(near_kernel, i, h),
        out_shape=jax.ShapeDtypeStruct((N, depth, width), BF),
        in_specs=whole(3),
        out_specs=whole(1)[0],
        **limits(0),
    )(rel, g, got)


def own_kernel(rel, g, from_up, from_down, kept, *sent):
    for j in (2, 1, 3, 0):
        total = dot(rel[0, j], g[...], 1, 0)
        total += from_up[j].astype(F32) + from_down[j].astype(F32)
        if j == 0:
            kept[...] = total
        else:
            sent[j - 1][...] = total.astype(BF)


def own(rel, g, from_up, from_down):
    depth, width = rel.shape[2], g.shape[1]
    block = jax.ShapeDtypeStruct((depth, width), BF)
    return pl.pallas_call(
        own_kernel,
        out_shape=(jax.ShapeDtypeStruct((depth, width), F32), block, block, block),
        in_specs=whole(4),
        out_specs=tuple(whole(4)),
        **limits(0),
    )(rel, g, from_up, from_down)


def total_kernel(kept, a, b, c, out):
    out[...] = kept[...] + (a[...].astype(F32) + b[...].astype(F32) + c[...].astype(F32))


def add_all(kept, *arrived):
    return pl.pallas_call(
        total_kernel,
        out_shape=jax.ShapeDtypeStruct(kept.shape, F32),
        in_specs=whole(4),
        out_specs=whole(1)[0],
        **limits(0),
    )(kept, *arrived)


def input_kernel(keys, place, g, *refs):
    pieces = dict(zip(keys, refs))
    kept, given, turned = refs[len(keys) :]
    turned[...] = g[...].T
    z, core = place[2], place[3]
    for (i, h), piece in pieces.items():
        depth = piece.shape[1]
        for j in (2 * h, 2 * h + 1):
            total = dot(piece[j % 2], turned[...], 1, 0)
            _, ahead, other = chip(place, i, j)
            to = lax.rem(ahead + N - z, N) * 2 + lax.rem(other, 2)
            rows = pl.ds(pl.multiple_of(to * depth, depth), depth)
            mine = other // 2 == core

            @pl.when(mine)
            def _():
                kept[rows] = total

            @pl.when(jnp.logical_not(mine))
            def _():
                given[rows] = total.astype(given.dtype)


def input_partial(place, g, pieces):
    count, width = g.shape
    rows = N * N * pieces[0, 0].shape[1] // 2
    return pl.pallas_call(
        functools.partial(input_kernel, tuple(pieces)),
        out_shape=(jax.ShapeDtypeStruct((rows, count), F32), jax.ShapeDtypeStruct((rows, count), BF)),
        in_specs=[pl.BlockSpec(memory_space=pltpu.SMEM)] + whole(1 + len(pieces)),
        out_specs=tuple(whole(2)),
        scratch_shapes=[pltpu.VMEM((width, count), BF)],
        **limits(10 * rows * width * count),
    )(place, g, *pieces.values())


def shards(tokens, weight, cotangent):
    row, col = lax.axis_index("row"), lax.axis_index("col")
    place = jnp.stack([row // N, row % N, col // 2, col % 2])
    depth = weight.shape[0]

    up, down, across = small(weight, -1), small(weight, 1), small(weight, 2)
    mine = turn(tokens)
    here = jnp.stack([mine, swap_core(mine)])
    got = spread_z(here)
    up, down, across = tied(up, down, across)
    w = {(0, 0): jnp.stack([weight, up]), (0, 1): jnp.stack([across, down])}
    w[1, 0] = big(w[0, 0], -1)
    w[3, 1] = big(w[0, 1], 1)
    w[1, 1] = big(w[0, 1], -1)
    w[3, 0] = big(w[0, 0], 1)
    got = jnp.concatenate([got, spread_z(got[:1])], axis=0)
    rel = arrange(place, here, got, swap_core(got))
    sums = add_sums(rel, None, {k: w[k] for k in ((0, 0), (0, 1), (1, 0), (3, 1))})
    w[2, 0] = big(w[1, 0], -1)
    w[2, 1] = big(w[3, 1], 1)
    sums = add_sums(rel, sums, {k: w[k] for k in ((1, 1), (3, 0))})
    activated, g = finish(rel, sums, cotangent, {k: w[k] for k in ((2, 0), (2, 1))})

    def far(h):
        block = rel[2, 2 * h : 2 * h + 2].reshape(2 * depth, -1)
        return dot(block, g, 1, 0).astype(BF).reshape(2, depth, -1)

    to_up, to_down = big(far(0), 1), big(far(1), -1)
    kept, given = input_partial(place, g, w)
    to_up, to_down, kept, given = tied(to_up, to_down, kept, given)
    up, down = big(near(1, 0, rel, g, to_up), 1), big(near(3, 1, rel, g, to_down), -1)
    total, sent_1, sent_2, sent_3 = own(rel, g, up, down)
    weight_grad = add_all(total, small(sent_2, 2), small(sent_1, 1), small(sent_3, -1))

    sums = (kept + swap_core(given).astype(F32)).reshape(N, 2 * depth, -1)
    sent = sums.astype(BF)
    z1, z3, z2 = shift_z(sent[1], 1), shift_z(sent[3], -1), shift_z(sent[2], 2)
    input_grad = (sums[0] + z1.astype(F32) + z2.astype(F32) + z3.astype(F32)).T.astype(BF)
    return (activated, input_grad, weight_grad)


def solution(mesh):
    specs = (P("row", "col"), P("row", "col"), P("row", "col"))
    return jax.shard_map(shards, mesh=mesh, in_specs=specs, out_specs=specs, check_vma=False)
```

```python
import functools

import jax
import jax.numpy as jnp
from jax import lax
from jax.experimental import pallas as pl
from jax.experimental.pallas import tpu as pltpu
from jax.sharding import PartitionSpec as P

N = 4
BF = jnp.bfloat16
F32 = jnp.float32


def shift(block, step, first):
    pairs = []
    for y in range(N):
        for x in range(N):
            for col in range(2 * N):
                if first == (col % 2 == 0):
                    to = y * N + (x + step) % N
                else:
                    to = (y + step) % N * N + x
                pairs.append(((y * N + x) * 2 * N + col, to * 2 * N + col))
    return lax.ppermute(block, ("row", "col"), pairs)


def small(block, step):
    return shift(block, step, True)


def big(block, step):
    return shift(block, step, False)


def shift_z(block, step):
    pairs = [(2 * z + core, 2 * ((z + step) % N) + core) for z in range(N) for core in range(2)]
    return lax.ppermute(block, "col", pairs)


def spread_z(block):
    pairs = [(2 * z + core, 2 * ((z + 1 - 2 * core) % N) + core) for z in range(N) for core in range(2)]
    return lax.ppermute(block, "col", pairs)


def swap_core(block):
    pairs = [(col, col ^ 1) for col in range(2 * N)]
    return lax.ppermute(block, "col", pairs)


def tied(*values):
    return lax.optimization_barrier(values)


def dot(a, b, ca, cb):
    return lax.dot_general(a, b, (((ca,), (cb,)), ((), ())), preferred_element_type=F32)


def whole(count):
    return [pl.BlockSpec(memory_space=pltpu.VMEM)] * count


def limits(flops):
    return dict(
        compiler_params=pltpu.CompilerParams(vmem_limit_bytes=24 * 2**20),
        cost_estimate=pl.CostEstimate(flops=flops, bytes_accessed=0, transcendentals=0),
    )


def turn_kernel(source, out):
    out[...] = source[...].T


def turn(block):
    return pl.pallas_call(
        turn_kernel,
        out_shape=jax.ShapeDtypeStruct(block.shape[::-1], block.dtype),
        in_specs=whole(1),
        out_specs=whole(1)[0],
        **limits(0),
    )(block)


def chip(place, i, j):
    turned = place[3] == 1
    y = lax.rem(place[0] + jnp.where(turned, j, i), N)
    x = lax.rem(place[1] + jnp.where(turned, i, j), N)
    return y * N + x, y, x


def arrange_kernel(place, here, got, other, out, sems):
    z, core = place[2], place[3]
    depth = out.shape[2]
    copies = []
    for i in range(N):
        for j in range(N):
            _, y, x = chip(place, i, j)
            ahead = lax.rem(y + N - z, N)
            rows = pl.ds(pl.multiple_of(lax.rem(x, 2) * depth, depth), depth)
            swapped = jnp.where(x // 2 == core, 0, 1)
            near = ahead == jnp.where(core == 0, 3, 1)
            two = ahead == 2
            choices = (
                (here, ahead == 0, swapped),
                (got, jnp.logical_or(near, jnp.logical_and(two, swapped == 0)), jnp.where(two, 2, swapped)),
                (
                    other,
                    jnp.logical_or(
                        ahead == jnp.where(core == 0, 1, 3), jnp.logical_and(two, swapped == 1)
                    ),
                    jnp.where(two, 2, 1 - swapped),
                ),
            )
            for source, chosen, at in choices:
                copy = pltpu.make_async_copy(source.at[at, rows], out.at[i, j], sems.at[i, j])
                pl.when(chosen)(copy.start)
            copies.append(pltpu.make_async_copy(here.at[0, rows], out.at[i, j], sems.at[i, j]))
    for copy in copies:
        copy.wait()


def arrange(place, here, got, other):
    _, rows, count = here.shape
    anywhere = pl.BlockSpec(memory_space=pl.ANY)
    return pl.pallas_call(
        arrange_kernel,
        out_shape=jax.ShapeDtypeStruct((N, N, rows // 2, count), BF),
        in_specs=[pl.BlockSpec(memory_space=pltpu.SMEM), anywhere, anywhere, anywhere],
        out_specs=whole(1)[0],
        scratch_shapes=[pltpu.SemaphoreType.DMA((N, N))],
        **limits(0),
    )(place, here, got, other)


def add_pieces(total, rel, pieces, tokens, columns):
    for (i, h), piece in pieces.items():
        left = rel[i, 2 * h : 2 * h + 2, :, tokens]
        right = piece[:, :, columns]
        term = dot(left.reshape(-1, left.shape[-1]), right.reshape(-1, right.shape[-1]), 0, 0)
        total = term if total is None else total + term
    return total


STEP, WIDE = 128, 768


def sum_kernel(keys, has_first, rel, *refs):
    first = refs[0] if has_first else None
    pieces = dict(zip(keys, refs[has_first : has_first + len(keys)]))
    out = refs[-1]
    for at in range(0, out.shape[0], STEP):
        for left in range(0, out.shape[1], WIDE):
            tokens, columns = slice(at, at + STEP), slice(left, left + WIDE)
            before = first[tokens, columns] if has_first else None
            out[tokens, columns] = add_pieces(before, rel, pieces, tokens, columns)


def add_sums(rel, first, pieces):
    shape = (rel.shape[-1], next(iter(pieces.values())).shape[-1])
    firsts = () if first is None else (first,)
    return pl.pallas_call(
        functools.partial(sum_kernel, tuple(pieces), len(firsts)),
        out_shape=jax.ShapeDtypeStruct(shape, F32),
        in_specs=whole(1 + len(firsts) + len(pieces)),
        out_specs=whole(1)[0],
        **limits(0),
    )(rel, *firsts, *pieces.values())


SCALE = 0.7978845608028654


def late_kernel(keys, rel, sums, cot, *refs):
    pieces = dict(zip(keys, refs))
    held, grad = refs[len(keys) :]
    for at in range(0, sums.shape[0], STEP):
        for left in range(0, sums.shape[1], WIDE):
            tokens, columns = slice(at, at + STEP), slice(left, left + WIDE)
            pre = add_pieces(sums[tokens, columns], rel, pieces, tokens, columns)
            square = pre * pre
            rise = 0.5 + 0.5 * jnp.tanh(pre * (SCALE + (SCALE * 0.044715) * square))
            held[tokens, columns] = pre * rise
            bend = pre * (2 * SCALE + (6 * SCALE * 0.044715) * square)
            slope = rise + rise * ((1.0 - rise) * bend)
            grad[tokens, columns] = (cot[tokens, columns].astype(F32) * slope).astype(BF)


def finish(rel, sums, cot, pieces):
    return pl.pallas_call(
        functools.partial(late_kernel, tuple(pieces)),
        out_shape=(jax.ShapeDtypeStruct(sums.shape, F32), jax.ShapeDtypeStruct(sums.shape, BF)),
        in_specs=whole(3 + len(pieces)),
        out_specs=tuple(whole(2)),
        **limits(0),
    )(rel, sums, cot, *pieces.values())


def own_kernel(rel, g, up_low, up_high, down_low, down_high, kept, *sent):
    for j in (2, 1, 3, 0):
        total = dot(rel[0, j], g[...], 1, 0)
        for low, high in ((up_low, up_high), (down_low, down_high)):
            total += (low if j < 2 else high)[j % 2].astype(F32)
        if j == 0:
            kept[...] = total
        else:
            sent[j - 1][...] = total.astype(BF)


def own(rel, g, *arrived):
    depth, width = rel.shape[2], g.shape[1]
    block = jax.ShapeDtypeStruct((depth, width), BF)
    return pl.pallas_call(
        own_kernel,
        out_shape=(jax.ShapeDtypeStruct((depth, width), F32), block, block, block),
        in_specs=whole(6),
        out_specs=tuple(whole(4)),
        **limits(0),
    )(rel, g, *arrived)


def total_kernel(kept, a, b, c, out):
    out[...] = kept[...] + (a[...].astype(F32) + b[...].astype(F32) + c[...].astype(F32))


def add_all(kept, *arrived):
    return pl.pallas_call(
        total_kernel,
        out_shape=jax.ShapeDtypeStruct(kept.shape, F32),
        in_specs=whole(4),
        out_specs=whole(1)[0],
        **limits(0),
    )(kept, *arrived)


def join_kernel(kept, a, b, c, out):
    total = kept[...] + (a[...].astype(F32) + b[...].astype(F32) + c[...].astype(F32))
    out[...] = total.astype(BF).T


def join(kept, *arrived):
    return pl.pallas_call(
        join_kernel,
        out_shape=jax.ShapeDtypeStruct(kept.shape[::-1], BF),
        in_specs=whole(4),
        out_specs=whole(1)[0],
        **limits(0),
    )(kept, *arrived)


def input_kernel(keys, place, g, *refs):
    pieces = dict(zip(keys, refs))
    kept, given, turned = refs[len(keys) :]
    turned[...] = g[...].T
    z, core = place[2], place[3]
    for (i, h), piece in pieces.items():
        depth = piece.shape[1]
        for j in (2 * h, 2 * h + 1):
            total = dot(piece[j % 2], turned[...], 1, 0)
            _, ahead, other = chip(place, i, j)
            to = lax.rem(ahead + N - z, N) * 2 + lax.rem(other, 2)
            rows = pl.ds(pl.multiple_of(to * depth, depth), depth)
            mine = other // 2 == core

            @pl.when(mine)
            def _():
                kept[rows] = total

            @pl.when(jnp.logical_not(mine))
            def _():
                given[rows] = total.astype(given.dtype)


def input_partial(place, g, pieces):
    count, width = g.shape
    rows = N * N * pieces[0, 0].shape[1] // 2
    return pl.pallas_call(
        functools.partial(input_kernel, tuple(pieces)),
        out_shape=(jax.ShapeDtypeStruct((rows, count), F32), jax.ShapeDtypeStruct((rows, count), BF)),
        in_specs=[pl.BlockSpec(memory_space=pltpu.SMEM)] + whole(1 + len(pieces)),
        out_specs=tuple(whole(2)),
        scratch_shapes=[pltpu.VMEM((width, count), BF)],
        **limits(0),
    )(place, g, *pieces.values())


def shards(tokens, weight, cotangent):
    row, col = lax.axis_index("row"), lax.axis_index("col")
    place = jnp.stack([row // N, row % N, col // 2, col % 2])
    depth = weight.shape[0]

    up, down, across = small(weight, -1), small(weight, 1), small(weight, 2)
    mine = turn(tokens)
    here = jnp.stack([mine, swap_core(mine)])
    got = spread_z(here)
    up, down, across = tied(up, down, across)
    w = {(0, 0): jnp.stack([weight, up]), (0, 1): jnp.stack([across, down])}
    w[1, 0] = big(w[0, 0], -1)
    w[3, 1] = big(w[0, 1], 1)
    w[1, 1] = big(w[0, 1], -1)
    w[3, 0] = big(w[0, 0], 1)
    got = jnp.concatenate([got, spread_z(got[:1])], axis=0)
    rel = arrange(place, here, got, swap_core(got))
    sums = add_sums(rel, None, {k: w[k] for k in ((0, 0), (0, 1), (1, 0), (3, 1))})
    w[2, 0] = big(w[1, 0], -1)
    w[2, 1] = big(w[3, 1], 1)
    sums = add_sums(rel, sums, {k: w[k] for k in ((1, 1), (3, 0))})
    held, g = finish(rel, sums, cotangent, {k: w[k] for k in ((2, 0), (2, 1))})

    def part(i, h):
        block = rel[i, 2 * h : 2 * h + 2].reshape(2 * depth, -1)
        return dot(block, g, 1, 0).reshape(2, depth, -1)

    to_up, to_down = big(part(2, 0).astype(BF), 1), big(part(2, 1).astype(BF), -1)
    up_high, down_low = big(part(1, 1).astype(BF), 1), big(part(3, 0).astype(BF), -1)
    kept, given = input_partial(place, g, w)
    to_up, to_down, kept, given, held = tied(to_up, to_down, kept, given, held)
    activated = held.astype(BF)
    up_low = (part(1, 0) + to_up.astype(F32)).astype(BF)
    down_high = (part(3, 1) + to_down.astype(F32)).astype(BF)
    up_low, down_high = big(up_low, 1), big(down_high, -1)

    sums = (kept + swap_core(given).astype(F32)).reshape(N, 2 * depth, -1)
    sent = sums.astype(BF)
    z1, z3, z2 = shift_z(sent[1], 1), shift_z(sent[3], -1), shift_z(sent[2], 2)

    total, sent_1, sent_2, sent_3 = own(rel, g, up_low, up_high, down_low, down_high)
    weight_grad = add_all(total, small(sent_2, 2), small(sent_1, 1), small(sent_3, -1))
    input_grad = join(sums[0], z1, z2, z3)
    return (activated, input_grad, weight_grad)


def solution(mesh):
    specs = (P("row", "col"), P("row", "col"), P("row", "col"))
    return jax.shard_map(shards, mesh=mesh, in_specs=specs, out_specs=specs, check_vma=False)
```

```python
import functools

import jax
import jax.numpy as jnp
from jax import lax
from jax.experimental import pallas as pl
from jax.experimental.pallas import tpu as pltpu
from jax.sharding import PartitionSpec as P

N = 4
BF = jnp.bfloat16
F32 = jnp.float32


def shift(block, step, first):
    pairs = []
    for y in range(N):
        for x in range(N):
            for col in range(2 * N):
                if first == (col % 2 == 0):
                    to = y * N + (x + step) % N
                else:
                    to = (y + step) % N * N + x
                pairs.append(((y * N + x) * 2 * N + col, to * 2 * N + col))
    return lax.ppermute(block, ("row", "col"), pairs)


def small(block, step):
    return shift(block, step, True)


def big(block, step):
    return shift(block, step, False)


def shift_z(block, step):
    pairs = [(2 * z + core, 2 * ((z + step) % N) + core) for z in range(N) for core in range(2)]
    return lax.ppermute(block, "col", pairs)


def spread_z(block):
    pairs = [(2 * z + core, 2 * ((z + 1 - 2 * core) % N) + core) for z in range(N) for core in range(2)]
    return lax.ppermute(block, "col", pairs)


def swap_core(block):
    pairs = [(col, col ^ 1) for col in range(2 * N)]
    return lax.ppermute(block, "col", pairs)


def tied(*values):
    return lax.optimization_barrier(values)


def dot(a, b, ca, cb):
    return lax.dot_general(a, b, (((ca,), (cb,)), ((), ())), preferred_element_type=F32)


def whole(count):
    return [pl.BlockSpec(memory_space=pltpu.VMEM)] * count


def limits(flops):
    return dict(
        compiler_params=pltpu.CompilerParams(vmem_limit_bytes=24 * 2**20),
        cost_estimate=pl.CostEstimate(flops=flops, bytes_accessed=0, transcendentals=0),
    )


def turn_kernel(source, out):
    out[...] = source[...].T


def turn(block):
    return pl.pallas_call(
        turn_kernel,
        out_shape=jax.ShapeDtypeStruct(block.shape[::-1], block.dtype),
        in_specs=whole(1),
        out_specs=whole(1)[0],
        **limits(0),
    )(block)


def chip(place, i, j):
    turned = place[3] == 1
    y = lax.rem(place[0] + jnp.where(turned, j, i), N)
    x = lax.rem(place[1] + jnp.where(turned, i, j), N)
    return y * N + x, y, x


def arrange_kernel(place, here, got, other, out, sems):
    z, core = place[2], place[3]
    depth = out.shape[2]
    copies = []
    for i in range(N):
        for j in range(N):
            _, y, x = chip(place, i, j)
            ahead = lax.rem(y + N - z, N)
            rows = pl.ds(pl.multiple_of(lax.rem(x, 2) * depth, depth), depth)
            swapped = jnp.where(x // 2 == core, 0, 1)
            near = ahead == jnp.where(core == 0, 3, 1)
            two = ahead == 2
            choices = (
                (here, ahead == 0, swapped),
                (got, jnp.logical_or(near, jnp.logical_and(two, swapped == 0)), jnp.where(two, 2, swapped)),
                (
                    other,
                    jnp.logical_or(
                        ahead == jnp.where(core == 0, 1, 3), jnp.logical_and(two, swapped == 1)
                    ),
                    jnp.where(two, 2, 1 - swapped),
                ),
            )
            for source, chosen, at in choices:
                copy = pltpu.make_async_copy(source.at[at, rows], out.at[i, j], sems.at[i, j])
                pl.when(chosen)(copy.start)
            copies.append(pltpu.make_async_copy(here.at[0, rows], out.at[i, j], sems.at[i, j]))
    for copy in copies:
        copy.wait()


def arrange(place, here, got, other):
    _, rows, count = here.shape
    anywhere = pl.BlockSpec(memory_space=pl.ANY)
    return pl.pallas_call(
        arrange_kernel,
        out_shape=jax.ShapeDtypeStruct((N, N, rows // 2, count), BF),
        in_specs=[pl.BlockSpec(memory_space=pltpu.SMEM), anywhere, anywhere, anywhere],
        out_specs=whole(1)[0],
        scratch_shapes=[pltpu.SemaphoreType.DMA((N, N))],
        **limits(0),
    )(place, here, got, other)


def add_pieces(total, rel, pieces, tokens, columns):
    for (i, h), piece in pieces.items():
        left = rel[i, 2 * h : 2 * h + 2, :, tokens]
        right = piece[:, :, columns]
        term = dot(left.reshape(-1, left.shape[-1]), right.reshape(-1, right.shape[-1]), 0, 0)
        total = term if total is None else total + term
    return total


STEP, WIDE = 128, 768


def sum_kernel(keys, has_first, rel, *refs):
    first = refs[0] if has_first else None
    pieces = dict(zip(keys, refs[has_first : has_first + len(keys)]))
    out = refs[-1]
    for at in range(0, out.shape[0], STEP):
        for left in range(0, out.shape[1], WIDE):
            tokens, columns = slice(at, at + STEP), slice(left, left + WIDE)
            before = first[tokens, columns] if has_first else None
            out[tokens, columns] = add_pieces(before, rel, pieces, tokens, columns)


def add_sums(rel, first, pieces):
    shape = (rel.shape[-1], next(iter(pieces.values())).shape[-1])
    firsts = () if first is None else (first,)
    return pl.pallas_call(
        functools.partial(sum_kernel, tuple(pieces), len(firsts)),
        out_shape=jax.ShapeDtypeStruct(shape, F32),
        in_specs=whole(1 + len(firsts) + len(pieces)),
        out_specs=whole(1)[0],
        **limits(0),
    )(rel, *firsts, *pieces.values())


SCALE = 0.7978845608028654


def late_kernel(keys, rel, sums, cot, *refs):
    pieces = dict(zip(keys, refs))
    held, grad = refs[len(keys) :]
    for at in range(0, sums.shape[0], STEP):
        for left in range(0, sums.shape[1], WIDE):
            tokens, columns = slice(at, at + STEP), slice(left, left + WIDE)
            pre = add_pieces(sums[tokens, columns], rel, pieces, tokens, columns)
            square = pre * pre
            rise = 0.5 + 0.5 * jnp.tanh(pre * (SCALE + (SCALE * 0.044715) * square))
            held[tokens, columns] = pre * rise
            bend = pre * (2 * SCALE + (6 * SCALE * 0.044715) * square)
            slope = rise + rise * ((1.0 - rise) * bend)
            grad[tokens, columns] = (cot[tokens, columns].astype(F32) * slope).astype(BF)


def finish(rel, sums, cot, pieces):
    return pl.pallas_call(
        functools.partial(late_kernel, tuple(pieces)),
        out_shape=(jax.ShapeDtypeStruct(sums.shape, F32), jax.ShapeDtypeStruct(sums.shape, BF)),
        in_specs=whole(3 + len(pieces)),
        out_specs=tuple(whole(2)),
        **limits(0),
    )(rel, sums, cot, *pieces.values())


def own_kernel(rel, g, up_low, up_high, down_low, down_high, kept, *sent):
    for j in (2, 1, 3, 0):
        total = dot(rel[0, j], g[...], 1, 0)
        for low, high in ((up_low, up_high), (down_low, down_high)):
            total += (low if j < 2 else high)[j % 2].astype(F32)
        if j == 0:
            kept[...] = total
        else:
            sent[j - 1][...] = total.astype(BF)


def own(rel, g, *arrived):
    depth, width = rel.shape[2], g.shape[1]
    block = jax.ShapeDtypeStruct((depth, width), BF)
    return pl.pallas_call(
        own_kernel,
        out_shape=(jax.ShapeDtypeStruct((depth, width), F32), block, block, block),
        in_specs=whole(6),
        out_specs=tuple(whole(4)),
        **limits(0),
    )(rel, g, *arrived)


def total_kernel(kept, a, b, c, out):
    out[...] = kept[...] + (a[...].astype(F32) + b[...].astype(F32) + c[...].astype(F32))


def add_all(kept, *arrived):
    return pl.pallas_call(
        total_kernel,
        out_shape=jax.ShapeDtypeStruct(kept.shape, F32),
        in_specs=whole(4),
        out_specs=whole(1)[0],
        **limits(0),
    )(kept, *arrived)


def join_kernel(kept, a, b, c, out):
    total = kept[...] + (a[...].astype(F32) + b[...].astype(F32) + c[...].astype(F32))
    out[...] = total.astype(BF).T


def join(kept, *arrived):
    return pl.pallas_call(
        join_kernel,
        out_shape=jax.ShapeDtypeStruct(kept.shape[::-1], BF),
        in_specs=whole(4),
        out_specs=whole(1)[0],
        **limits(0),
    )(kept, *arrived)


def input_kernel(keys, place, g, *refs):
    pieces = dict(zip(keys, refs))
    kept, given, turned = refs[len(keys) :]
    turned[...] = g[...].T
    z, core = place[2], place[3]
    for (i, h), piece in pieces.items():
        depth = piece.shape[1]
        for j in (2 * h, 2 * h + 1):
            total = dot(piece[j % 2], turned[...], 1, 0)
            _, ahead, other = chip(place, i, j)
            to = lax.rem(ahead + N - z, N) * 2 + lax.rem(other, 2)
            rows = pl.ds(pl.multiple_of(to * depth, depth), depth)
            mine = other // 2 == core

            @pl.when(mine)
            def _():
                kept[rows] = total

            @pl.when(jnp.logical_not(mine))
            def _():
                given[rows] = total.astype(given.dtype)


def input_partial(place, g, pieces):
    count, width = g.shape
    rows = N * N * pieces[0, 0].shape[1] // 2
    return pl.pallas_call(
        functools.partial(input_kernel, tuple(pieces)),
        out_shape=(jax.ShapeDtypeStruct((rows, count), F32), jax.ShapeDtypeStruct((rows, count), BF)),
        in_specs=[pl.BlockSpec(memory_space=pltpu.SMEM)] + whole(1 + len(pieces)),
        out_specs=tuple(whole(2)),
        scratch_shapes=[pltpu.VMEM((width, count), BF)],
        **limits(0),
    )(place, g, *pieces.values())


def shards(tokens, weight, cotangent):
    row, col = lax.axis_index("row"), lax.axis_index("col")
    place = jnp.stack([row // N, row % N, col // 2, col % 2])
    depth = weight.shape[0]

    across, up, down = small(weight, 2), small(weight, -1), small(weight, 1)
    mine = turn(tokens)
    here = jnp.stack([mine, swap_core(mine)])
    got = spread_z(here)
    across, up, down = tied(across, up, down)
    w = {(0, 0): jnp.stack([weight, up]), (0, 1): jnp.stack([across, down])}
    w[1, 0] = big(w[0, 0], -1)
    w[3, 1] = big(w[0, 1], 1)
    w[1, 1] = big(w[0, 1], -1)
    w[3, 0] = big(w[0, 0], 1)
    got = jnp.concatenate([got, spread_z(got[:1])], axis=0)
    rel = arrange(place, here, got, swap_core(got))
    sums = add_sums(rel, None, {k: w[k] for k in ((0, 0), (0, 1), (1, 0), (3, 1))})
    w[2, 0] = big(w[1, 0], -1)
    w[2, 1] = big(w[3, 1], 1)
    sums = add_sums(rel, sums, {k: w[k] for k in ((1, 1), (3, 0))})
    held, g = finish(rel, sums, cotangent, {k: w[k] for k in ((2, 0), (2, 1))})

    def part(i, h):
        block = rel[i, 2 * h : 2 * h + 2].reshape(2 * depth, -1)
        return dot(block, g, 1, 0).reshape(2, depth, -1)

    to_up, to_down = big(part(2, 0).astype(BF), 1), big(part(2, 1).astype(BF), -1)
    up_high, down_low = big(part(1, 1).astype(BF), 1), big(part(3, 0).astype(BF), -1)
    kept, given = input_partial(place, g, w)
    to_up, to_down, kept, given, held = tied(to_up, to_down, kept, given, held)
    activated = held.astype(BF)
    up_low = (part(1, 0) + to_up.astype(F32)).astype(BF)
    down_high = (part(3, 1) + to_down.astype(F32)).astype(BF)
    up_low, down_high = big(up_low, 1), big(down_high, -1)

    sums = (kept + swap_core(given).astype(F32)).reshape(N, 2 * depth, -1)
    sent = sums.astype(BF)
    z1, z3, z2 = shift_z(sent[1], 1), shift_z(sent[3], -1), shift_z(sent[2], 2)

    total, sent_1, sent_2, sent_3 = own(rel, g, up_low, up_high, down_low, down_high)
    weight_grad = add_all(total, small(sent_2, 2), small(sent_1, 1), small(sent_3, -1))
    input_grad = join(sums[0], z1, z2, z3)
    return (activated, input_grad, weight_grad)


def solution(mesh):
    specs = (P("row", "col"), P("row", "col"), P("row", "col"))
    return jax.shard_map(shards, mesh=mesh, in_specs=specs, out_specs=specs, check_vma=False)
```

```python
import functools

import jax
import jax.numpy as jnp
from jax import lax
from jax.experimental import pallas as pl
from jax.experimental.pallas import tpu as pltpu
from jax.sharding import PartitionSpec as P

N = 4
BF = jnp.bfloat16
F32 = jnp.float32


def shift(block, step, first):
    pairs = []
    for y in range(N):
        for x in range(N):
            for col in range(2 * N):
                if first == (col % 2 == 0):
                    to = y * N + (x + step) % N
                else:
                    to = (y + step) % N * N + x
                pairs.append(((y * N + x) * 2 * N + col, to * 2 * N + col))
    return lax.ppermute(block, ("row", "col"), pairs)


def small(block, step):
    return shift(block, step, True)


def big(block, step):
    return shift(block, step, False)


def shift_z(block, step):
    pairs = [(2 * z + core, 2 * ((z + step) % N) + core) for z in range(N) for core in range(2)]
    return lax.ppermute(block, "col", pairs)


def spread_z(block):
    pairs = [(2 * z + core, 2 * ((z + 1 - 2 * core) % N) + core) for z in range(N) for core in range(2)]
    return lax.ppermute(block, "col", pairs)


def swap_core(block):
    pairs = [(col, col ^ 1) for col in range(2 * N)]
    return lax.ppermute(block, "col", pairs)


def tied(*values):
    return lax.optimization_barrier(values)


def dot(a, b, ca, cb):
    return lax.dot_general(a, b, (((ca,), (cb,)), ((), ())), preferred_element_type=F32)


def whole(count):
    return [pl.BlockSpec(memory_space=pltpu.VMEM)] * count


def limits(flops):
    return dict(
        compiler_params=pltpu.CompilerParams(vmem_limit_bytes=24 * 2**20),
        cost_estimate=pl.CostEstimate(flops=flops, bytes_accessed=0, transcendentals=0),
    )


def turn_kernel(source, out):
    out[...] = source[...].T


def turn(block):
    return pl.pallas_call(
        turn_kernel,
        out_shape=jax.ShapeDtypeStruct(block.shape[::-1], block.dtype),
        in_specs=whole(1),
        out_specs=whole(1)[0],
        **limits(0),
    )(block)


def chip(place, i, j):
    turned = place[3] == 1
    y = lax.rem(place[0] + jnp.where(turned, j, i), N)
    x = lax.rem(place[1] + jnp.where(turned, i, j), N)
    return y * N + x, y, x


def arrange_kernel(place, here, got, other, out, sems):
    z, core = place[2], place[3]
    depth = out.shape[2]
    copies = []
    for i in range(N):
        for j in range(N):
            _, y, x = chip(place, i, j)
            ahead = lax.rem(y + N - z, N)
            rows = pl.ds(pl.multiple_of(lax.rem(x, 2) * depth, depth), depth)
            swapped = jnp.where(x // 2 == core, 0, 1)
            near = ahead == jnp.where(core == 0, 3, 1)
            two = ahead == 2
            choices = (
                (here, ahead == 0, swapped),
                (got, jnp.logical_or(near, jnp.logical_and(two, swapped == 0)), jnp.where(two, 2, swapped)),
                (
                    other,
                    jnp.logical_or(
                        ahead == jnp.where(core == 0, 1, 3), jnp.logical_and(two, swapped == 1)
                    ),
                    jnp.where(two, 2, 1 - swapped),
                ),
            )
            for source, chosen, at in choices:
                copy = pltpu.make_async_copy(source.at[at, rows], out.at[i, j], sems.at[i, j])
                pl.when(chosen)(copy.start)
            copies.append(pltpu.make_async_copy(here.at[0, rows], out.at[i, j], sems.at[i, j]))
    for copy in copies:
        copy.wait()


def arrange(place, here, got, other):
    _, rows, count = here.shape
    anywhere = pl.BlockSpec(memory_space=pl.ANY)
    return pl.pallas_call(
        arrange_kernel,
        out_shape=jax.ShapeDtypeStruct((N, N, rows // 2, count), BF),
        in_specs=[pl.BlockSpec(memory_space=pltpu.SMEM), anywhere, anywhere, anywhere],
        out_specs=whole(1)[0],
        scratch_shapes=[pltpu.SemaphoreType.DMA((N, N))],
        **limits(0),
    )(place, here, got, other)


def add_pieces(total, rel, pieces, tokens, columns):
    for (i, h), piece in pieces.items():
        left = rel[i, 2 * h : 2 * h + 2, :, tokens]
        right = piece[:, :, columns]
        term = dot(left.reshape(-1, left.shape[-1]), right.reshape(-1, right.shape[-1]), 0, 0)
        total = term if total is None else total + term
    return total


STEP, WIDE = 128, 768


def sum_kernel(keys, has_first, rel, *refs):
    first = refs[0] if has_first else None
    pieces = dict(zip(keys, refs[has_first : has_first + len(keys)]))
    out = refs[-1]
    for at in range(0, out.shape[0], STEP):
        for left in range(0, out.shape[1], WIDE):
            tokens, columns = slice(at, at + STEP), slice(left, left + WIDE)
            before = first[tokens, columns] if has_first else None
            out[tokens, columns] = add_pieces(before, rel, pieces, tokens, columns)


def add_sums(rel, first, pieces):
    shape = (rel.shape[-1], next(iter(pieces.values())).shape[-1])
    firsts = () if first is None else (first,)
    return pl.pallas_call(
        functools.partial(sum_kernel, tuple(pieces), len(firsts)),
        out_shape=jax.ShapeDtypeStruct(shape, F32),
        in_specs=whole(1 + len(firsts) + len(pieces)),
        out_specs=whole(1)[0],
        **limits(0),
    )(rel, *firsts, *pieces.values())


SCALE = 0.7978845608028654


def late_kernel(keys, rel, sums, cot, *refs):
    pieces = dict(zip(keys, refs))
    held, grad = refs[len(keys) :]
    for at in range(0, sums.shape[0], STEP):
        for left in range(0, sums.shape[1], WIDE):
            tokens, columns = slice(at, at + STEP), slice(left, left + WIDE)
            pre = add_pieces(sums[tokens, columns], rel, pieces, tokens, columns)
            square = pre * pre
            rise = 0.5 + 0.5 * jnp.tanh(pre * (SCALE + (SCALE * 0.044715) * square))
            held[tokens, columns] = pre * rise
            bend = pre * (2 * SCALE + (6 * SCALE * 0.044715) * square)
            slope = rise + rise * ((1.0 - rise) * bend)
            grad[tokens, columns] = (cot[tokens, columns].astype(F32) * slope).astype(BF)


def finish(rel, sums, cot, pieces):
    return pl.pallas_call(
        functools.partial(late_kernel, tuple(pieces)),
        out_shape=(jax.ShapeDtypeStruct(sums.shape, F32), jax.ShapeDtypeStruct(sums.shape, BF)),
        in_specs=whole(3 + len(pieces)),
        out_specs=tuple(whole(2)),
        **limits(0),
    )(rel, sums, cot, *pieces.values())


def second_kernel(i, h, rel, g, got, out):
    for k in (0, 1):
        out[k] = (dot(rel[i, 2 * h + k], g[...], 1, 0) + got[k].astype(F32)).astype(BF)


def second(i, h, rel, g, got):
    return pl.pallas_call(
        functools.partial(second_kernel, i, h),
        out_shape=jax.ShapeDtypeStruct(got.shape, BF),
        in_specs=whole(3),
        out_specs=whole(1)[0],
        **limits(0),
    )(rel, g, got)


def mix_kernel(kept, other, base, one, two, three):
    rows = base.shape[0]
    for k, out in enumerate((base, one, two, three)):
        at = slice(k * rows, (k + 1) * rows)
        out[...] = (kept[at] + other[at].astype(F32)).astype(out.dtype)


def mix(kept, other):
    rows, count = kept.shape[0] // N, kept.shape[1]
    block = jax.ShapeDtypeStruct((rows, count), BF)
    return pl.pallas_call(
        mix_kernel,
        out_shape=(jax.ShapeDtypeStruct((rows, count), F32), block, block, block),
        in_specs=whole(2),
        out_specs=tuple(whole(4)),
        **limits(0),
    )(kept, other)


def own_kernel(rel, g, up_low, up_high, down_low, down_high, kept, *sent):
    for j in (2, 1, 3, 0):
        total = dot(rel[0, j], g[...], 1, 0)
        for low, high in ((up_low, up_high), (down_low, down_high)):
            total += (low if j < 2 else high)[j % 2].astype(F32)
        if j == 0:
            kept[...] = total
        else:
            sent[j - 1][...] = total.astype(BF)


def own(rel, g, *arrived):
    depth, width = rel.shape[2], g.shape[1]
    block = jax.ShapeDtypeStruct((depth, width), BF)
    return pl.pallas_call(
        own_kernel,
        out_shape=(jax.ShapeDtypeStruct((depth, width), F32), block, block, block),
        in_specs=whole(6),
        out_specs=tuple(whole(4)),
        **limits(0),
    )(rel, g, *arrived)


def total_kernel(kept, a, b, c, out):
    out[...] = kept[...] + (a[...].astype(F32) + b[...].astype(F32) + c[...].astype(F32))


def add_all(kept, *arrived):
    return pl.pallas_call(
        total_kernel,
        out_shape=jax.ShapeDtypeStruct(kept.shape, F32),
        in_specs=whole(4),
        out_specs=whole(1)[0],
        **limits(0),
    )(kept, *arrived)


def join_kernel(kept, a, b, c, out):
    total = kept[...] + (a[...].astype(F32) + b[...].astype(F32) + c[...].astype(F32))
    out[...] = total.astype(BF).T


def join(kept, *arrived):
    return pl.pallas_call(
        join_kernel,
        out_shape=jax.ShapeDtypeStruct(kept.shape[::-1], BF),
        in_specs=whole(4),
        out_specs=whole(1)[0],
        **limits(0),
    )(kept, *arrived)


def input_kernel(keys, place, g, *refs):
    pieces = dict(zip(keys, refs))
    kept, given, turned = refs[len(keys) :]
    turned[...] = g[...].T
    z, core = place[2], place[3]
    for (i, h), piece in pieces.items():
        depth = piece.shape[1]
        for j in (2 * h, 2 * h + 1):
            total = dot(piece[j % 2], turned[...], 1, 0)
            _, ahead, other = chip(place, i, j)
            to = lax.rem(ahead + N - z, N) * 2 + lax.rem(other, 2)
            rows = pl.ds(pl.multiple_of(to * depth, depth), depth)
            mine = other // 2 == core

            @pl.when(mine)
            def _():
                kept[rows] = total

            @pl.when(jnp.logical_not(mine))
            def _():
                given[rows] = total.astype(given.dtype)


def input_partial(place, g, pieces):
    count, width = g.shape
    rows = N * N * pieces[0, 0].shape[1] // 2
    return pl.pallas_call(
        functools.partial(input_kernel, tuple(pieces)),
        out_shape=(jax.ShapeDtypeStruct((rows, count), F32), jax.ShapeDtypeStruct((rows, count), BF)),
        in_specs=[pl.BlockSpec(memory_space=pltpu.SMEM)] + whole(1 + len(pieces)),
        out_specs=tuple(whole(2)),
        scratch_shapes=[pltpu.VMEM((width, count), BF)],
        **limits(0),
    )(place, g, *pieces.values())


def shards(tokens, weight, cotangent):
    row, col = lax.axis_index("row"), lax.axis_index("col")
    place = jnp.stack([row // N, row % N, col // 2, col % 2])
    depth = weight.shape[0]

    across, up, down = small(weight, 2), small(weight, -1), small(weight, 1)
    mine = turn(tokens)
    here = jnp.stack([mine, swap_core(mine)])
    got = spread_z(here)
    across, up, down = tied(across, up, down)
    w = {(0, 0): jnp.stack([weight, up]), (0, 1): jnp.stack([across, down])}
    w[1, 0] = big(w[0, 0], -1)
    w[3, 1] = big(w[0, 1], 1)
    w[1, 1] = big(w[0, 1], -1)
    w[3, 0] = big(w[0, 0], 1)
    got = jnp.concatenate([got, spread_z(got[:1])], axis=0)
    rel = arrange(place, here, got, swap_core(got))
    sums = add_sums(rel, None, {k: w[k] for k in ((0, 0), (0, 1), (1, 0), (3, 1))})
    w[2, 0] = big(w[1, 0], -1)
    w[2, 1] = big(w[3, 1], 1)
    sums = add_sums(rel, sums, {k: w[k] for k in ((1, 1), (3, 0))})
    held, g = finish(rel, sums, cotangent, {k: w[k] for k in ((2, 0), (2, 1))})

    def part(i, h):
        block = rel[i, 2 * h : 2 * h + 2].reshape(2 * depth, -1)
        return dot(block, g, 1, 0).reshape(2, depth, -1)

    to_up, to_down = big(part(2, 0).astype(BF), 1), big(part(2, 1).astype(BF), -1)
    up_high, down_low = big(part(1, 1).astype(BF), 1), big(part(3, 0).astype(BF), -1)
    kept, given = input_partial(place, g, w)
    to_up, to_down, kept, given, held = tied(to_up, to_down, kept, given, held)
    activated = held.astype(BF)
    up_low, down_high = big(second(1, 0, rel, g, to_up), 1), big(second(3, 1, rel, g, to_down), -1)

    base, z1, z2, z3 = mix(kept, swap_core(given))
    z1, z3, z2 = shift_z(z1, 1), shift_z(z3, -1), shift_z(z2, 2)
    total, sent_1, sent_2, sent_3 = own(rel, g, up_low, up_high, down_low, down_high)
    weight_grad = add_all(total, small(sent_2, 2), small(sent_1, 1), small(sent_3, -1))
    input_grad = join(base, z1, z2, z3)
    return (activated, input_grad, weight_grad)


def solution(mesh):
    specs = (P("row", "col"), P("row", "col"), P("row", "col"))
    return jax.shard_map(shards, mesh=mesh, in_specs=specs, out_specs=specs, check_vma=False)
```

```python
import functools

import jax
import jax.numpy as jnp
from jax import lax
from jax.experimental import pallas as pl
from jax.experimental.pallas import tpu as pltpu
from jax.sharding import PartitionSpec as P

N = 4
BF = jnp.bfloat16
F32 = jnp.float32


def shift(block, step, first):
    pairs = []
    for y in range(N):
        for x in range(N):
            for col in range(2 * N):
                if first == (col % 2 == 0):
                    to = y * N + (x + step) % N
                else:
                    to = (y + step) % N * N + x
                pairs.append(((y * N + x) * 2 * N + col, to * 2 * N + col))
    return lax.ppermute(block, ("row", "col"), pairs)


def small(block, step):
    return shift(block, step, True)


def big(block, step):
    return shift(block, step, False)


def shift_z(block, step):
    pairs = [(2 * z + core, 2 * ((z + step) % N) + core) for z in range(N) for core in range(2)]
    return lax.ppermute(block, "col", pairs)


def spread_z(block, step=1):
    pairs = [(2 * z + core, 2 * ((z + step - 2 * step * core) % N) + core) for z in range(N) for core in range(2)]
    return lax.ppermute(block, "col", pairs)


def swap_core(block):
    pairs = [(col, col ^ 1) for col in range(2 * N)]
    return lax.ppermute(block, "col", pairs)


def tied(*values):
    return lax.optimization_barrier(values)


def dot(a, b, ca, cb):
    return lax.dot_general(a, b, (((ca,), (cb,)), ((), ())), preferred_element_type=F32)


def whole(count):
    return [pl.BlockSpec(memory_space=pltpu.VMEM)] * count


def limits(flops):
    return dict(
        compiler_params=pltpu.CompilerParams(vmem_limit_bytes=24 * 2**20),
        cost_estimate=pl.CostEstimate(flops=flops, bytes_accessed=0, transcendentals=0),
    )


def turn_kernel(source, out):
    out[...] = source[...].T


def turn(block):
    return pl.pallas_call(
        turn_kernel,
        out_shape=jax.ShapeDtypeStruct(block.shape[::-1], block.dtype),
        in_specs=whole(1),
        out_specs=whole(1)[0],
        **limits(0),
    )(block)


def chip(place, i, j):
    turned = place[3] == 1
    y = lax.rem(place[0] + jnp.where(turned, j, i), N)
    x = lax.rem(place[1] + jnp.where(turned, i, j), N)
    return y * N + x, y, x


def arrange_kernel(place, here, got, other, out, sems):
    z, core = place[2], place[3]
    depth = out.shape[2]
    copies = []
    for i in range(N):
        for j in range(N):
            _, y, x = chip(place, i, j)
            ahead = lax.rem(y + N - z, N)
            rows = pl.ds(pl.multiple_of(lax.rem(x, 2) * depth, depth), depth)
            swapped = jnp.where(x // 2 == core, 0, 1)
            near = ahead == jnp.where(core == 0, 3, 1)
            two = ahead == 2
            choices = (
                (here, ahead == 0, swapped),
                (got, jnp.logical_or(near, jnp.logical_and(two, swapped == 0)), jnp.where(two, 2, swapped)),
                (
                    other,
                    jnp.logical_or(
                        ahead == jnp.where(core == 0, 1, 3), jnp.logical_and(two, swapped == 1)
                    ),
                    jnp.where(two, 2, 1 - swapped),
                ),
            )
            for source, chosen, at in choices:
                copy = pltpu.make_async_copy(source.at[at, rows], out.at[i, j], sems.at[i, j])
                pl.when(chosen)(copy.start)
            copies.append(pltpu.make_async_copy(here.at[0, rows], out.at[i, j], sems.at[i, j]))
    for copy in copies:
        copy.wait()


def arrange(place, here, got, other):
    _, rows, count = here.shape
    anywhere = pl.BlockSpec(memory_space=pl.ANY)
    return pl.pallas_call(
        arrange_kernel,
        out_shape=jax.ShapeDtypeStruct((N, N, rows // 2, count), BF),
        in_specs=[pl.BlockSpec(memory_space=pltpu.SMEM), anywhere, anywhere, anywhere],
        out_specs=whole(1)[0],
        scratch_shapes=[pltpu.SemaphoreType.DMA((N, N))],
        **limits(0),
    )(place, here, got, other)


def add_pieces(total, rel, pieces, tokens, columns):
    for (i, h), piece in pieces.items():
        left = rel[i, 2 * h : 2 * h + 2, :, tokens]
        right = piece[:, :, columns]
        term = dot(left.reshape(-1, left.shape[-1]), right.reshape(-1, right.shape[-1]), 0, 0)
        total = term if total is None else total + term
    return total


STEP, WIDE = 128, 768


def sum_kernel(keys, has_first, rel, *refs):
    first = refs[0] if has_first else None
    pieces = dict(zip(keys, refs[has_first : has_first + len(keys)]))
    out = refs[-1]
    for at in range(0, out.shape[0], STEP):
        for left in range(0, out.shape[1], WIDE):
            tokens, columns = slice(at, at + STEP), slice(left, left + WIDE)
            before = first[tokens, columns] if has_first else None
            out[tokens, columns] = add_pieces(before, rel, pieces, tokens, columns)


def add_sums(rel, first, pieces):
    shape = (rel.shape[-1], next(iter(pieces.values())).shape[-1])
    firsts = () if first is None else (first,)
    return pl.pallas_call(
        functools.partial(sum_kernel, tuple(pieces), len(firsts)),
        out_shape=jax.ShapeDtypeStruct(shape, F32),
        in_specs=whole(1 + len(firsts) + len(pieces)),
        out_specs=whole(1)[0],
        **limits(0),
    )(rel, *firsts, *pieces.values())


SCALE = 0.7978845608028654


def late_kernel(keys, rel, sums, cot, *refs):
    pieces = dict(zip(keys, refs))
    held, grad = refs[len(keys) :]
    for at in range(0, sums.shape[0], STEP):
        for left in range(0, sums.shape[1], WIDE):
            tokens, columns = slice(at, at + STEP), slice(left, left + WIDE)
            pre = add_pieces(sums[tokens, columns], rel, pieces, tokens, columns)
            square = pre * pre
            rise = 0.5 + 0.5 * jnp.tanh(pre * (SCALE + (SCALE * 0.044715) * square))
            held[tokens, columns] = pre * rise
            bend = pre * (2 * SCALE + (6 * SCALE * 0.044715) * square)
            slope = rise + rise * ((1.0 - rise) * bend)
            grad[tokens, columns] = (cot[tokens, columns].astype(F32) * slope).astype(BF)


def finish(rel, sums, cot, pieces):
    return pl.pallas_call(
        functools.partial(late_kernel, tuple(pieces)),
        out_shape=(jax.ShapeDtypeStruct(sums.shape, F32), jax.ShapeDtypeStruct(sums.shape, BF)),
        in_specs=whole(3 + len(pieces)),
        out_specs=tuple(whole(2)),
        **limits(0),
    )(rel, sums, cot, *pieces.values())


def second_kernel(i, h, rel, g, got, out):
    for k in (0, 1):
        out[k] = (dot(rel[i, 2 * h + k], g[...], 1, 0) + got[k].astype(F32)).astype(BF)


def second(i, h, rel, g, got):
    return pl.pallas_call(
        functools.partial(second_kernel, i, h),
        out_shape=jax.ShapeDtypeStruct(got.shape, BF),
        in_specs=whole(3),
        out_specs=whole(1)[0],
        **limits(0),
    )(rel, g, got)


def mix_kernel(place, kept, other, base, one, two, three):
    rows = base.shape[0]
    core = place[3]
    for k, out in ((0, base), (1 + 2 * core, one), (2, two), (3 - 2 * core, three)):
        at = pl.ds(pl.multiple_of(k * rows, rows), rows)
        out[...] = (kept[at] + other[at].astype(F32)).astype(out.dtype)


def mix(place, kept, other):
    rows, count = kept.shape[0] // N, kept.shape[1]
    block = jax.ShapeDtypeStruct((rows, count), BF)
    return pl.pallas_call(
        mix_kernel,
        out_shape=(jax.ShapeDtypeStruct((rows, count), F32), block, block, block),
        in_specs=[pl.BlockSpec(memory_space=pltpu.SMEM)] + whole(2),
        out_specs=tuple(whole(4)),
        **limits(0),
    )(place, kept, other)


def own_kernel(rel, g, up_low, up_high, down_low, down_high, kept, *sent):
    for j in (2, 1, 3, 0):
        total = dot(rel[0, j], g[...], 1, 0)
        for low, high in ((up_low, up_high), (down_low, down_high)):
            total += (low if j < 2 else high)[j % 2].astype(F32)
        if j == 0:
            kept[...] = total
        else:
            sent[j - 1][...] = total.astype(BF)


def own(rel, g, *arrived):
    depth, width = rel.shape[2], g.shape[1]
    block = jax.ShapeDtypeStruct((depth, width), BF)
    return pl.pallas_call(
        own_kernel,
        out_shape=(jax.ShapeDtypeStruct((depth, width), F32), block, block, block),
        in_specs=whole(6),
        out_specs=tuple(whole(4)),
        **limits(0),
    )(rel, g, *arrived)


def total_kernel(kept, a, b, c, out):
    out[...] = kept[...] + (a[...].astype(F32) + b[...].astype(F32) + c[...].astype(F32))


def add_all(kept, *arrived):
    return pl.pallas_call(
        total_kernel,
        out_shape=jax.ShapeDtypeStruct(kept.shape, F32),
        in_specs=whole(4),
        out_specs=whole(1)[0],
        **limits(0),
    )(kept, *arrived)


def join_kernel(kept, a, b, c, out):
    total = kept[...] + (a[...].astype(F32) + b[...].astype(F32) + c[...].astype(F32))
    out[...] = total.astype(BF).T


def join(kept, *arrived):
    return pl.pallas_call(
        join_kernel,
        out_shape=jax.ShapeDtypeStruct(kept.shape[::-1], BF),
        in_specs=whole(4),
        out_specs=whole(1)[0],
        **limits(0),
    )(kept, *arrived)


def input_kernel(keys, place, g, *refs):
    pieces = dict(zip(keys, refs))
    kept, given, turned = refs[len(keys) :]
    turned[...] = g[...].T
    z, core = place[2], place[3]
    for (i, h), piece in pieces.items():
        depth = piece.shape[1]
        for j in (2 * h, 2 * h + 1):
            total = dot(piece[j % 2], turned[...], 1, 0)
            _, ahead, other = chip(place, i, j)
            to = lax.rem(ahead + N - z, N) * 2 + lax.rem(other, 2)
            rows = pl.ds(pl.multiple_of(to * depth, depth), depth)
            mine = other // 2 == core

            @pl.when(mine)
            def _():
                kept[rows] = total

            @pl.when(jnp.logical_not(mine))
            def _():
                given[rows] = total.astype(given.dtype)


def input_partial(place, g, pieces):
    count, width = g.shape
    rows = N * N * pieces[0, 0].shape[1] // 2
    return pl.pallas_call(
        functools.partial(input_kernel, tuple(pieces)),
        out_shape=(jax.ShapeDtypeStruct((rows, count), F32), jax.ShapeDtypeStruct((rows, count), BF)),
        in_specs=[pl.BlockSpec(memory_space=pltpu.SMEM)] + whole(1 + len(pieces)),
        out_specs=tuple(whole(2)),
        scratch_shapes=[pltpu.VMEM((width, count), BF)],
        **limits(0),
    )(place, g, *pieces.values())


def shards(tokens, weight, cotangent):
    row, col = lax.axis_index("row"), lax.axis_index("col")
    place = jnp.stack([row // N, row % N, col // 2, col % 2])
    depth = weight.shape[0]

    across, up, down = small(weight, 2), small(weight, -1), small(weight, 1)
    mine = turn(tokens)
    here = jnp.stack([mine, swap_core(mine)])
    got = spread_z(here)
    across, up, down = tied(across, up, down)
    w = {(0, 0): jnp.stack([weight, up]), (0, 1): jnp.stack([across, down])}
    w[1, 0] = big(w[0, 0], -1)
    w[3, 1] = big(w[0, 1], 1)
    w[1, 1] = big(w[0, 1], -1)
    w[3, 0] = big(w[0, 0], 1)
    got = jnp.concatenate([got, spread_z(got[:1])], axis=0)
    rel = arrange(place, here, got, swap_core(got))
    sums = add_sums(rel, None, {k: w[k] for k in ((0, 0), (0, 1), (1, 0), (3, 1))})
    w[2, 0] = big(w[1, 0], -1)
    w[2, 1] = big(w[3, 1], 1)
    sums = add_sums(rel, sums, {k: w[k] for k in ((1, 1), (3, 0))})
    held, g = finish(rel, sums, cotangent, {k: w[k] for k in ((2, 0), (2, 1))})

    def part(i, h):
        block = rel[i, 2 * h : 2 * h + 2].reshape(2 * depth, -1)
        return dot(block, g, 1, 0).reshape(2, depth, -1)

    to_up, to_down = big(part(2, 0).astype(BF), 1), big(part(2, 1).astype(BF), -1)
    up_high, down_low = big(part(1, 1).astype(BF), 1), big(part(3, 0).astype(BF), -1)
    kept, given = input_partial(place, g, w)
    to_up, to_down, kept, given, held = tied(to_up, to_down, kept, given, held)
    activated = held.astype(BF)
    up_low, down_high = big(second(1, 0, rel, g, to_up), 1), big(second(3, 1, rel, g, to_down), -1)

    base, z1, z2, z3 = mix(place, kept, swap_core(given))
    z1, z2, z3 = spread_z(z1), shift_z(z2, 2), spread_z(z3, -1)
    total, sent_1, sent_2, sent_3 = own(rel, g, up_low, up_high, down_low, down_high)
    weight_grad = add_all(total, small(sent_2, 2), small(sent_1, 1), small(sent_3, -1))
    input_grad = join(base, z1, z2, z3)
    return (activated, input_grad, weight_grad)


def solution(mesh):
    specs = (P("row", "col"), P("row", "col"), P("row", "col"))
    return jax.shard_map(shards, mesh=mesh, in_specs=specs, out_specs=specs, check_vma=False)
```

```python
import functools

import jax
import jax.numpy as jnp
from jax import lax
from jax.experimental import pallas as pl
from jax.experimental.pallas import tpu as pltpu
from jax.sharding import PartitionSpec as P

N = 4
BF = jnp.bfloat16
F32 = jnp.float32


def shift(block, step, first):
    pairs = []
    for y in range(N):
        for x in range(N):
            for col in range(2 * N):
                if first == (col % 2 == 0):
                    to = y * N + (x + step) % N
                else:
                    to = (y + step) % N * N + x
                pairs.append(((y * N + x) * 2 * N + col, to * 2 * N + col))
    return lax.ppermute(block, ("row", "col"), pairs)


def small(block, step):
    return shift(block, step, True)


def big(block, step):
    return shift(block, step, False)


def shift_z(block, step):
    pairs = [(2 * z + core, 2 * ((z + step) % N) + core) for z in range(N) for core in range(2)]
    return lax.ppermute(block, "col", pairs)


def spread_z(block):
    pairs = [(2 * z + core, 2 * ((z + 1 - 2 * core) % N) + core) for z in range(N) for core in range(2)]
    return lax.ppermute(block, "col", pairs)


def swap_core(block):
    pairs = [(col, col ^ 1) for col in range(2 * N)]
    return lax.ppermute(block, "col", pairs)


def tied(*values):
    return lax.optimization_barrier(values)


def dot(a, b, ca, cb):
    return lax.dot_general(a, b, (((ca,), (cb,)), ((), ())), preferred_element_type=F32)


def whole(count):
    return [pl.BlockSpec(memory_space=pltpu.VMEM)] * count


def limits(flops):
    return dict(
        compiler_params=pltpu.CompilerParams(vmem_limit_bytes=24 * 2**20),
        cost_estimate=pl.CostEstimate(flops=flops, bytes_accessed=0, transcendentals=0),
    )


def turn_kernel(source, out):
    out[...] = source[...].T


def turn(block):
    return pl.pallas_call(
        turn_kernel,
        out_shape=jax.ShapeDtypeStruct(block.shape[::-1], block.dtype),
        in_specs=whole(1),
        out_specs=whole(1)[0],
        **limits(0),
    )(block)


def chip(place, i, j):
    turned = place[3] == 1
    y = lax.rem(place[0] + jnp.where(turned, j, i), N)
    x = lax.rem(place[1] + jnp.where(turned, i, j), N)
    return y * N + x, y, x


def arrange_kernel(place, here, got, other, out, sems):
    z, core = place[2], place[3]
    depth = out.shape[2]
    copies = []
    for i in range(N):
        for j in range(N):
            _, y, x = chip(place, i, j)
            ahead = lax.rem(y + N - z, N)
            rows = pl.ds(pl.multiple_of(lax.rem(x, 2) * depth, depth), depth)
            swapped = jnp.where(x // 2 == core, 0, 1)
            near = ahead == jnp.where(core == 0, 3, 1)
            two = ahead == 2
            choices = (
                (here, ahead == 0, swapped),
                (got, jnp.logical_or(near, jnp.logical_and(two, swapped == 0)), jnp.where(two, 2, swapped)),
                (
                    other,
                    jnp.logical_or(
                        ahead == jnp.where(core == 0, 1, 3), jnp.logical_and(two, swapped == 1)
                    ),
                    jnp.where(two, 2, 1 - swapped),
                ),
            )
            for source, chosen, at in choices:
                copy = pltpu.make_async_copy(source.at[at, rows], out.at[i, j], sems.at[i, j])
                pl.when(chosen)(copy.start)
            copies.append(pltpu.make_async_copy(here.at[0, rows], out.at[i, j], sems.at[i, j]))
    for copy in copies:
        copy.wait()


def arrange(place, here, got, other):
    _, rows, count = here.shape
    anywhere = pl.BlockSpec(memory_space=pl.ANY)
    return pl.pallas_call(
        arrange_kernel,
        out_shape=jax.ShapeDtypeStruct((N, N, rows // 2, count), BF),
        in_specs=[pl.BlockSpec(memory_space=pltpu.SMEM), anywhere, anywhere, anywhere],
        out_specs=whole(1)[0],
        scratch_shapes=[pltpu.SemaphoreType.DMA((N, N))],
        **limits(0),
    )(place, here, got, other)


def add_pieces(total, rel, pieces, tokens, columns):
    for (i, h), piece in pieces.items():
        left = rel[i, 2 * h : 2 * h + 2, :, tokens]
        right = piece[:, :, columns]
        term = dot(left.reshape(-1, left.shape[-1]), right.reshape(-1, right.shape[-1]), 0, 0)
        total = term if total is None else total + term
    return total


STEP, WIDE = 128, 768


def sum_kernel(keys, has_first, rel, *refs):
    first = refs[0] if has_first else None
    pieces = dict(zip(keys, refs[has_first : has_first + len(keys)]))
    out = refs[-1]
    for at in range(0, out.shape[0], STEP):
        for left in range(0, out.shape[1], WIDE):
            tokens, columns = slice(at, at + STEP), slice(left, left + WIDE)
            before = first[tokens, columns] if has_first else None
            out[tokens, columns] = add_pieces(before, rel, pieces, tokens, columns)


def add_sums(rel, first, pieces):
    shape = (rel.shape[-1], next(iter(pieces.values())).shape[-1])
    firsts = () if first is None else (first,)
    return pl.pallas_call(
        functools.partial(sum_kernel, tuple(pieces), len(firsts)),
        out_shape=jax.ShapeDtypeStruct(shape, F32),
        in_specs=whole(1 + len(firsts) + len(pieces)),
        out_specs=whole(1)[0],
        **limits(0),
    )(rel, *firsts, *pieces.values())


SCALE = 0.7978845608028654


def late_kernel(keys, rel, sums, cot, *refs):
    pieces = dict(zip(keys, refs))
    held, grad = refs[len(keys) :]
    for at in range(0, sums.shape[0], STEP):
        for left in range(0, sums.shape[1], WIDE):
            tokens, columns = slice(at, at + STEP), slice(left, left + WIDE)
            pre = add_pieces(sums[tokens, columns], rel, pieces, tokens, columns)
            square = pre * pre
            rise = 0.5 + 0.5 * jnp.tanh(pre * (SCALE + (SCALE * 0.044715) * square))
            held[tokens, columns] = pre * rise
            bend = pre * (2 * SCALE + (6 * SCALE * 0.044715) * square)
            slope = rise + rise * ((1.0 - rise) * bend)
            grad[tokens, columns] = (cot[tokens, columns].astype(F32) * slope).astype(BF)


def finish(rel, sums, cot, pieces):
    return pl.pallas_call(
        functools.partial(late_kernel, tuple(pieces)),
        out_shape=(jax.ShapeDtypeStruct(sums.shape, F32), jax.ShapeDtypeStruct(sums.shape, BF)),
        in_specs=whole(3 + len(pieces)),
        out_specs=tuple(whole(2)),
        **limits(0),
    )(rel, sums, cot, *pieces.values())


def second_kernel(i, h, rel, g, got, out):
    for k in (0, 1):
        out[k] = (dot(rel[i, 2 * h + k], g[...], 1, 0) + got[k].astype(F32)).astype(BF)


def second(i, h, rel, g, got):
    return pl.pallas_call(
        functools.partial(second_kernel, i, h),
        out_shape=jax.ShapeDtypeStruct(got.shape, BF),
        in_specs=whole(3),
        out_specs=whole(1)[0],
        **limits(0),
    )(rel, g, got)


def mix_kernel(kept, other, base, one, two, three):
    rows = base.shape[0]
    for k, out in enumerate((base, one, two, three)):
        at = slice(k * rows, (k + 1) * rows)
        out[...] = (kept[at] + other[at].astype(F32)).astype(out.dtype)


def mix(kept, other):
    rows, count = kept.shape[0] // N, kept.shape[1]
    block = jax.ShapeDtypeStruct((rows, count), BF)
    return pl.pallas_call(
        mix_kernel,
        out_shape=(jax.ShapeDtypeStruct((rows, count), F32), block, block, block),
        in_specs=whole(2),
        out_specs=tuple(whole(4)),
        **limits(0),
    )(kept, other)


def own_sums(j, rel, g, up_low, up_high, down_low, down_high):
    total = dot(rel[0, j], g[...], 1, 0)
    for low, high in ((up_low, up_high), (down_low, down_high)):
        total += (low if j < 2 else high)[j % 2].astype(F32)
    return total


def own_kernel(steps, *refs):
    for j, out in zip(steps, refs[6:]):
        out[...] = own_sums(j, *refs[:6]).astype(out.dtype)


def own(steps, rel, g, *arrived):
    shape = (rel.shape[2], g.shape[1])
    return pl.pallas_call(
        functools.partial(own_kernel, steps),
        out_shape=tuple(jax.ShapeDtypeStruct(shape, BF if j else F32) for j in steps),
        in_specs=whole(6),
        out_specs=tuple(whole(len(steps))),
        **limits(0),
    )(rel, g, *arrived)


def total_kernel(kept, a, b, c, out):
    out[...] = kept[...] + (a[...].astype(F32) + b[...].astype(F32) + c[...].astype(F32))


def add_all(kept, *arrived):
    return pl.pallas_call(
        total_kernel,
        out_shape=jax.ShapeDtypeStruct(kept.shape, F32),
        in_specs=whole(4),
        out_specs=whole(1)[0],
        **limits(0),
    )(kept, *arrived)


def join_kernel(kept, a, b, c, out):
    total = kept[...] + (a[...].astype(F32) + b[...].astype(F32) + c[...].astype(F32))
    out[...] = total.astype(BF).T


def join(kept, *arrived):
    return pl.pallas_call(
        join_kernel,
        out_shape=jax.ShapeDtypeStruct(kept.shape[::-1], BF),
        in_specs=whole(4),
        out_specs=whole(1)[0],
        **limits(0),
    )(kept, *arrived)


def input_kernel(keys, place, g, *refs):
    pieces = dict(zip(keys, refs))
    kept, given, turned = refs[len(keys) :]
    turned[...] = g[...].T
    z, core = place[2], place[3]
    for (i, h), piece in pieces.items():
        depth = piece.shape[1]
        for j in (2 * h, 2 * h + 1):
            total = dot(piece[j % 2], turned[...], 1, 0)
            _, ahead, other = chip(place, i, j)
            to = lax.rem(ahead + N - z, N) * 2 + lax.rem(other, 2)
            rows = pl.ds(pl.multiple_of(to * depth, depth), depth)
            mine = other // 2 == core

            @pl.when(mine)
            def _():
                kept[rows] = total

            @pl.when(jnp.logical_not(mine))
            def _():
                given[rows] = total.astype(given.dtype)


def input_partial(place, g, pieces):
    count, width = g.shape
    rows = N * N * pieces[0, 0].shape[1] // 2
    return pl.pallas_call(
        functools.partial(input_kernel, tuple(pieces)),
        out_shape=(jax.ShapeDtypeStruct((rows, count), F32), jax.ShapeDtypeStruct((rows, count), BF)),
        in_specs=[pl.BlockSpec(memory_space=pltpu.SMEM)] + whole(1 + len(pieces)),
        out_specs=tuple(whole(2)),
        scratch_shapes=[pltpu.VMEM((width, count), BF)],
        **limits(0),
    )(place, g, *pieces.values())


def shards(tokens, weight, cotangent):
    row, col = lax.axis_index("row"), lax.axis_index("col")
    place = jnp.stack([row // N, row % N, col // 2, col % 2])
    depth = weight.shape[0]

    across, up, down = small(weight, 2), small(weight, -1), small(weight, 1)
    mine = turn(tokens)
    here = jnp.stack([mine, swap_core(mine)])
    got = spread_z(here)
    across, up, down = tied(across, up, down)
    w = {(0, 0): jnp.stack([weight, up]), (0, 1): jnp.stack([across, down])}
    w[1, 0] = big(w[0, 0], -1)
    w[3, 1] = big(w[0, 1], 1)
    w[1, 1] = big(w[0, 1], -1)
    w[3, 0] = big(w[0, 0], 1)
    got = jnp.concatenate([got, spread_z(got[:1])], axis=0)
    rel = arrange(place, here, got, swap_core(got))
    sums = add_sums(rel, None, {k: w[k] for k in ((0, 0), (0, 1), (1, 0), (3, 1))})
    w[2, 0] = big(w[1, 0], -1)
    w[2, 1] = big(w[3, 1], 1)
    sums = add_sums(rel, sums, {k: w[k] for k in ((1, 1), (3, 0))})
    held, g = finish(rel, sums, cotangent, {k: w[k] for k in ((2, 0), (2, 1))})

    def part(i, h):
        block = rel[i, 2 * h : 2 * h + 2].reshape(2 * depth, -1)
        return dot(block, g, 1, 0).reshape(2, depth, -1)

    to_up, to_down = big(part(2, 0).astype(BF), 1), big(part(2, 1).astype(BF), -1)
    up_high, down_low = big(part(1, 1).astype(BF), 1), big(part(3, 0).astype(BF), -1)
    kept, given = input_partial(place, g, w)
    to_up, to_down, kept, given, held = tied(to_up, to_down, kept, given, held)
    activated = held.astype(BF)
    up_low, down_high = big(second(1, 0, rel, g, to_up), 1), big(second(3, 1, rel, g, to_down), -1)

    base, z1, z2, z3 = mix(kept, swap_core(given))
    z1, z3, z2 = shift_z(z1, 1), shift_z(z3, -1), shift_z(z2, 2)
    arrived = (up_low, up_high, down_low, down_high)
    (sent_2,) = own((2,), rel, g, *arrived)
    sent_1, sent_3, total = own((1, 3, 0), rel, g, *arrived)
    weight_grad = add_all(total, small(sent_2, 2), small(sent_1, 1), small(sent_3, -1))
    input_grad = join(base, z1, z2, z3)
    return (activated, input_grad, weight_grad)


def solution(mesh):
    specs = (P("row", "col"), P("row", "col"), P("row", "col"))
    return jax.shard_map(shards, mesh=mesh, in_specs=specs, out_specs=specs, check_vma=False)
```

```python
import functools

import jax
import jax.numpy as jnp
from jax import lax
from jax.experimental import pallas as pl
from jax.experimental.pallas import tpu as pltpu
from jax.sharding import PartitionSpec as P

N = 4
BF = jnp.bfloat16
F32 = jnp.float32


def shift(block, step, first):
    pairs = []
    for y in range(N):
        for x in range(N):
            for col in range(2 * N):
                if first == (col % 2 == 0):
                    to = y * N + (x + step) % N
                else:
                    to = (y + step) % N * N + x
                pairs.append(((y * N + x) * 2 * N + col, to * 2 * N + col))
    return lax.ppermute(block, ("row", "col"), pairs)


def small(block, step):
    return shift(block, step, True)


def big(block, step):
    return shift(block, step, False)


def shift_z(block, step):
    pairs = [(2 * z + core, 2 * ((z + step) % N) + core) for z in range(N) for core in range(2)]
    return lax.ppermute(block, "col", pairs)


def spread_z(block):
    pairs = [(2 * z + core, 2 * ((z + 1 - 2 * core) % N) + core) for z in range(N) for core in range(2)]
    return lax.ppermute(block, "col", pairs)


def swap_core(block):
    pairs = [(col, col ^ 1) for col in range(2 * N)]
    return lax.ppermute(block, "col", pairs)


def tied(*values):
    return lax.optimization_barrier(values)


def dot(a, b, ca, cb):
    return lax.dot_general(a, b, (((ca,), (cb,)), ((), ())), preferred_element_type=F32)


def whole(count):
    return [pl.BlockSpec(memory_space=pltpu.VMEM)] * count


def limits(flops):
    return dict(
        compiler_params=pltpu.CompilerParams(vmem_limit_bytes=24 * 2**20),
        cost_estimate=pl.CostEstimate(flops=flops, bytes_accessed=0, transcendentals=0),
    )


def turn_kernel(source, out):
    out[...] = source[...].T


def turn(block):
    return pl.pallas_call(
        turn_kernel,
        out_shape=jax.ShapeDtypeStruct(block.shape[::-1], block.dtype),
        in_specs=whole(1),
        out_specs=whole(1)[0],
        **limits(0),
    )(block)


def chip(place, i, j):
    turned = place[3] == 1
    y = lax.rem(place[0] + jnp.where(turned, j, i), N)
    x = lax.rem(place[1] + jnp.where(turned, i, j), N)
    return y * N + x, y, x


def arrange_kernel(place, here, got, other, out, sems):
    z, core = place[2], place[3]
    depth = out.shape[2]
    copies = []
    for i in range(N):
        for j in range(N):
            _, y, x = chip(place, i, j)
            ahead = lax.rem(y + N - z, N)
            rows = pl.ds(pl.multiple_of(lax.rem(x, 2) * depth, depth), depth)
            swapped = jnp.where(x // 2 == core, 0, 1)
            near = ahead == jnp.where(core == 0, 3, 1)
            two = ahead == 2
            choices = (
                (here, ahead == 0, swapped),
                (got, jnp.logical_or(near, jnp.logical_and(two, swapped == 0)), jnp.where(two, 2, swapped)),
                (
                    other,
                    jnp.logical_or(
                        ahead == jnp.where(core == 0, 1, 3), jnp.logical_and(two, swapped == 1)
                    ),
                    jnp.where(two, 2, 1 - swapped),
                ),
            )
            for source, chosen, at in choices:
                copy = pltpu.make_async_copy(source.at[at, rows], out.at[i, j], sems.at[i, j])
                pl.when(chosen)(copy.start)
            copies.append(pltpu.make_async_copy(here.at[0, rows], out.at[i, j], sems.at[i, j]))
    for copy in copies:
        copy.wait()


def arrange(place, here, got, other):
    _, rows, count = here.shape
    anywhere = pl.BlockSpec(memory_space=pl.ANY)
    return pl.pallas_call(
        arrange_kernel,
        out_shape=jax.ShapeDtypeStruct((N, N, rows // 2, count), BF),
        in_specs=[pl.BlockSpec(memory_space=pltpu.SMEM), anywhere, anywhere, anywhere],
        out_specs=whole(1)[0],
        scratch_shapes=[pltpu.SemaphoreType.DMA((N, N))],
        **limits(0),
    )(place, here, got, other)


def add_pieces(total, rel, pieces, tokens, columns):
    for (i, h), piece in pieces.items():
        left = rel[i, 2 * h : 2 * h + 2, :, tokens]
        right = piece[:, :, columns]
        term = dot(left.reshape(-1, left.shape[-1]), right.reshape(-1, right.shape[-1]), 0, 0)
        total = term if total is None else total + term
    return total


STEP, WIDE = 128, 768


def sum_kernel(keys, has_first, rel, *refs):
    first = refs[0] if has_first else None
    pieces = dict(zip(keys, refs[has_first : has_first + len(keys)]))
    out = refs[-1]
    for at in range(0, out.shape[0], STEP):
        for left in range(0, out.shape[1], WIDE):
            tokens, columns = slice(at, at + STEP), slice(left, left + WIDE)
            before = first[tokens, columns] if has_first else None
            out[tokens, columns] = add_pieces(before, rel, pieces, tokens, columns)


def add_sums(rel, first, pieces):
    shape = (rel.shape[-1], next(iter(pieces.values())).shape[-1])
    firsts = () if first is None else (first,)
    return pl.pallas_call(
        functools.partial(sum_kernel, tuple(pieces), len(firsts)),
        out_shape=jax.ShapeDtypeStruct(shape, F32),
        in_specs=whole(1 + len(firsts) + len(pieces)),
        out_specs=whole(1)[0],
        **limits(0),
    )(rel, *firsts, *pieces.values())


SCALE = 0.7978845608028654


def late_kernel(keys, rel, sums, cot, *refs):
    pieces = dict(zip(keys, refs))
    held, grad = refs[len(keys) :]
    for at in range(0, sums.shape[0], STEP):
        for left in range(0, sums.shape[1], WIDE):
            tokens, columns = slice(at, at + STEP), slice(left, left + WIDE)
            pre = add_pieces(sums[tokens, columns], rel, pieces, tokens, columns)
            square = pre * pre
            rise = 0.5 + 0.5 * jnp.tanh(pre * (SCALE + (SCALE * 0.044715) * square))
            held[tokens, columns] = pre * rise
            bend = pre * (2 * SCALE + (6 * SCALE * 0.044715) * square)
            slope = rise + rise * ((1.0 - rise) * bend)
            grad[tokens, columns] = (cot[tokens, columns].astype(F32) * slope).astype(BF)


def finish(rel, sums, cot, pieces):
    return pl.pallas_call(
        functools.partial(late_kernel, tuple(pieces)),
        out_shape=(jax.ShapeDtypeStruct(sums.shape, F32), jax.ShapeDtypeStruct(sums.shape, BF)),
        in_specs=whole(3 + len(pieces)),
        out_specs=tuple(whole(2)),
        **limits(0),
    )(rel, sums, cot, *pieces.values())


def second_kernel(i, h, rel, g, got, out):
    for k in (0, 1):
        out[k] = (dot(rel[i, 2 * h + k], g[...], 1, 0) + got[k].astype(F32)).astype(BF)


def second(i, h, rel, g, got):
    return pl.pallas_call(
        functools.partial(second_kernel, i, h),
        out_shape=jax.ShapeDtypeStruct(got.shape, BF),
        in_specs=whole(3),
        out_specs=whole(1)[0],
        **limits(0),
    )(rel, g, got)


def mix_kernel(kept, other, base, one, two, three):
    rows = base.shape[0]
    for k, out in enumerate((base, one, two, three)):
        at = slice(k * rows, (k + 1) * rows)
        out[...] = (kept[at] + other[at].astype(F32)).astype(out.dtype)


def mix(kept, other):
    rows, count = kept.shape[0] // N, kept.shape[1]
    block = jax.ShapeDtypeStruct((rows, count), BF)
    return pl.pallas_call(
        mix_kernel,
        out_shape=(jax.ShapeDtypeStruct((rows, count), F32), block, block, block),
        in_specs=whole(2),
        out_specs=tuple(whole(4)),
        **limits(0),
    )(kept, other)


def own_sums(j, rel, g, up_low, up_high, down_low, down_high):
    total = dot(rel[0, j], g[...], 1, 0)
    for low, high in ((up_low, up_high), (down_low, down_high)):
        total += (low if j < 2 else high)[j % 2].astype(F32)
    return total


def own_kernel(steps, *refs):
    for j, out in zip(steps, refs[6:]):
        out[...] = own_sums(j, *refs[:6]).astype(out.dtype)


def own(steps, rel, g, *arrived):
    shape = (rel.shape[2], g.shape[1])
    return pl.pallas_call(
        functools.partial(own_kernel, steps),
        out_shape=tuple(jax.ShapeDtypeStruct(shape, BF if j else F32) for j in steps),
        in_specs=whole(6),
        out_specs=tuple(whole(len(steps))),
        **limits(0),
    )(rel, g, *arrived)


def total_kernel(kept, a, b, c, out):
    out[...] = kept[...] + (a[...].astype(F32) + b[...].astype(F32) + c[...].astype(F32))


def add_all(kept, *arrived):
    return pl.pallas_call(
        total_kernel,
        out_shape=jax.ShapeDtypeStruct(kept.shape, F32),
        in_specs=whole(4),
        out_specs=whole(1)[0],
        **limits(0),
    )(kept, *arrived)


def join_kernel(kept, a, b, c, out):
    total = kept[...] + (a[...].astype(F32) + b[...].astype(F32) + c[...].astype(F32))
    out[...] = total.astype(BF).T


def join(kept, *arrived):
    return pl.pallas_call(
        join_kernel,
        out_shape=jax.ShapeDtypeStruct(kept.shape[::-1], BF),
        in_specs=whole(4),
        out_specs=whole(1)[0],
        **limits(0),
    )(kept, *arrived)


def input_kernel(keys, place, g, *refs):
    pieces = dict(zip(keys, refs))
    kept, given, turned = refs[len(keys) :]
    turned[...] = g[...].T
    z, core = place[2], place[3]
    for (i, h), piece in pieces.items():
        depth = piece.shape[1]
        for j in (2 * h, 2 * h + 1):
            total = dot(piece[j % 2], turned[...], 1, 0)
            _, ahead, other = chip(place, i, j)
            to = lax.rem(ahead + N - z, N) * 2 + lax.rem(other, 2)
            rows = pl.ds(pl.multiple_of(to * depth, depth), depth)
            mine = other // 2 == core

            @pl.when(mine)
            def _():
                kept[rows] = total

            @pl.when(jnp.logical_not(mine))
            def _():
                given[rows] = total.astype(given.dtype)


def input_partial(place, g, pieces):
    count, width = g.shape
    rows = N * N * pieces[0, 0].shape[1] // 2
    return pl.pallas_call(
        functools.partial(input_kernel, tuple(pieces)),
        out_shape=(jax.ShapeDtypeStruct((rows, count), F32), jax.ShapeDtypeStruct((rows, count), BF)),
        in_specs=[pl.BlockSpec(memory_space=pltpu.SMEM)] + whole(1 + len(pieces)),
        out_specs=tuple(whole(2)),
        scratch_shapes=[pltpu.VMEM((width, count), BF)],
        **limits(0),
    )(place, g, *pieces.values())


def shards(tokens, weight, cotangent):
    row, col = lax.axis_index("row"), lax.axis_index("col")
    place = jnp.stack([row // N, row % N, col // 2, col % 2])
    depth = weight.shape[0]

    across, up, down = small(weight, 2), small(weight, -1), small(weight, 1)
    mine = turn(tokens)
    here = jnp.stack([mine, swap_core(mine)])
    got = spread_z(here)
    across, up, down = tied(across, up, down)
    w = {(0, 0): jnp.stack([weight, up]), (0, 1): jnp.stack([across, down])}
    w[1, 0] = big(w[0, 0], -1)
    w[3, 1] = big(w[0, 1], 1)
    w[1, 1] = big(w[0, 1], -1)
    w[3, 0] = big(w[0, 0], 1)
    got = jnp.concatenate([got, spread_z(got[:1])], axis=0)
    rel = arrange(place, here, got, swap_core(got))
    sums = add_sums(rel, None, {k: w[k] for k in ((0, 0), (0, 1), (1, 0), (3, 1))})
    w[2, 0] = big(w[1, 0], -1)
    w[2, 1] = big(w[3, 1], 1)
    sums = add_sums(rel, sums, {k: w[k] for k in ((1, 1), (3, 0))})
    held, g = finish(rel, sums, cotangent, {k: w[k] for k in ((2, 0), (2, 1))})

    def part(i, h):
        block = rel[i, 2 * h : 2 * h + 2].reshape(2 * depth, -1)
        return dot(block, g, 1, 0).reshape(2, depth, -1)

    to_up, to_down = big(part(2, 0).astype(BF), 1), big(part(2, 1).astype(BF), -1)
    up_high, down_low = big(part(1, 1).astype(BF), 1), big(part(3, 0).astype(BF), -1)
    kept, given = input_partial(place, g, w)
    to_up, to_down, kept, given, held = tied(to_up, to_down, kept, given, held)
    activated = held.astype(BF)
    up_low, down_high = big(second(1, 0, rel, g, to_up), 1), big(second(3, 1, rel, g, to_down), -1)

    base, z1, z2, z3 = mix(kept, swap_core(given))
    z1, z3, z2 = shift_z(z1, 1), shift_z(z3, -1), shift_z(z2, 2)
    arrived = (up_low, up_high, down_low, down_high)
    (sent_2,) = own((2,), rel, g, *arrived)
    sent_1, sent_3 = own((1, 3), rel, g, *arrived)
    (total,) = own((0,), rel, g, *arrived)
    weight_grad = add_all(total, small(sent_2, 2), small(sent_1, 1), small(sent_3, -1))
    input_grad = join(base, z1, z2, z3)
    return (activated, input_grad, weight_grad)


def solution(mesh):
    specs = (P("row", "col"), P("row", "col"), P("row", "col"))
    return jax.shard_map(shards, mesh=mesh, in_specs=specs, out_specs=specs, check_vma=False)
```
